256 devices in a mesh: wide: 16 (over z, x_lo), narrow: 16 (over x_hi, y, core).
Axes of the slice: x: 4 (x_hi: 2, x_lo: 2; x = x_hi * 2 + x_lo), y: 4, z: 8, core: 2. Of those that a mesh axis runs over, the one named last changes fastest.
Arguments:
- panel: float32 [16, 2097152], P(None, ('wide', 'narrow'))
- signs: int32 [2097152], P(('wide', 'narrow')), may hold values from -1 to 1, as said below
- samples: int32 [16384], replicated, may hold values from 0 to 2097151, as said below
Outputs:
- mixed: float32 [16, 2097152], P(None, ('wide', 'narrow'))
- gram: float32 [16, 16], replicated
The draws below stay inside these ranges and needn't reach their ends.
Inputs may be any that keep to these rules, and one draw needn't show every extreme that they name: `signs`: every entry is -1 or 1. `samples`: indices may repeat; the first is 0 and the last is 2097151.
All inputs are finite; a program needn't handle non-finite values.
Results may differ from the reference program's by a relative error of at most 0.000098.
Values sent between devices are 32-bit elements; how exact they have to be, the bound alone decides.
No kernel may reach another device: no remote copies, remote signals or barrier semaphores. Data moves between devices by JAX's collectives and lax.ppermute only.
A program may use at most 64 MiB of HBM per device.

```python
import jax
import jax.numpy as jnp
from jax import lax

PANEL = 16
R_DEV = 8192
ROWS = 2097152
SAMPLES = 16384


def draw_panel(key, part):
    key = jax.random.fold_in(key, 11)
    scale_key, value_key = jax.random.split(key, 2)
    column_scale = jnp.exp(jax.random.uniform(scale_key, (PANEL, 1), jnp.float32, -1.2, 1.1))
    values = jax.random.normal(value_key, (PANEL, ROWS), jnp.float32)
    return values * column_scale


def draw_signs(key, part):
    key = jax.random.fold_in(key, 23)
    return 2 * jax.random.randint(key, (ROWS,), 0, 2, jnp.int32) - 1


def draw_samples(key, part):
    key = jax.random.fold_in(key, 37)
    pick_key, local_key = jax.random.split(key)
    devices = ROWS // R_DEV
    weights = devices - 1 + 2 * jnp.arange(devices, dtype=jnp.int32)
    bounds = jnp.cumsum(weights)
    ticket = jax.random.randint(pick_key, (SAMPLES,), 0, bounds[-1], jnp.int32)
    owner = jnp.sum((ticket[:, None] >= bounds[None, :]).astype(jnp.int32), axis=1)
    local = jax.random.randint(local_key, (SAMPLES,), 0, R_DEV, jnp.int32)
    chosen = owner * R_DEV + local
    chosen = chosen.at[0].set(0)
    return chosen.at[SAMPLES - 1].set(ROWS - 1)


def setup_inputs(seed: int = 0) -> dict:
    key_of = jax.random.split(jax.random.key(seed), 4)
    return {
        "panel": draw_panel(jax.random.fold_in(key_of[3], 71), 0),
        "signs": draw_signs(jax.random.fold_in(key_of[3], 71), 0),
        "samples": draw_samples(jax.random.fold_in(key_of[3], 71), 0),
    }


def hadamard(order):
    bits = order.bit_length() - 1
    first = jnp.arange(order, dtype=jnp.int32)[:, None]
    second = jnp.arange(order, dtype=jnp.int32)[None, :]
    parity = jnp.zeros((order, order), jnp.int32)
    for level in range(bits):
        parity = parity + (first >> level & 1) * (second >> level & 1)
    return jnp.where(parity % 2 == 0, 1.0, -1.0).astype(jnp.float32)

def reference(panel, signs, samples):
    devices = ROWS // R_DEV
    blocks = R_DEV // 128
    flipped = panel * signs.astype(jnp.float32)[None, :]
    shaped = flipped.reshape(PANEL, devices, blocks, 128)
    high = lax.Precision.HIGHEST
    shaped = jnp.einsum('pdbc,ec->pdbe', shaped, hadamard(128), precision=high)
    shaped = jnp.einsum('pdbc,eb->pdec', shaped, hadamard(blocks), precision=high)
    shaped = jnp.einsum('pdbc,ed->pebc', shaped, hadamard(devices), precision=high)
    mixed = shaped.reshape(PANEL, ROWS) * (1.0 / jnp.sqrt(jnp.float32(ROWS)))
    picked = jnp.take(mixed, samples.astype(jnp.int32), axis=1)
    gram = jnp.dot(picked, picked.T, precision=high, preferred_element_type=jnp.float32) / jnp.float32(SAMPLES)
    return (mixed, gram)
```

```python
import functools

import jax
import jax.numpy as jnp
from jax import lax
from jax.experimental import pallas as pl
from jax.experimental.pallas import tpu as pltpu
from jax.sharding import PartitionSpec as P

COLUMNS = 16
LANES = 128
BLOCKS = 64
DEVICES = 256
LOCAL_ROWS = BLOCKS * LANES
SAMPLES = 16384
BOTH = ("wide", "narrow")
NT = (((1,), (1,)), ((), ()))
HIGH = lax.Precision.HIGHEST
VMEM = pl.BlockSpec(memory_space=pltpu.VMEM)
SMEM = pl.BlockSpec(memory_space=pltpu.SMEM)
LIMIT = 32 * 1024 * 1024


def hadamard(rows, columns):
    first = lax.broadcasted_iota(jnp.int32, (rows, columns), 0)
    second = lax.broadcasted_iota(jnp.int32, (rows, columns), 1)
    bits = first & second
    bits = bits ^ (bits >> 4)
    bits = bits ^ (bits >> 2)
    bits = bits ^ (bits >> 1)
    return jnp.where((bits & 1) == 0, 1.0, -1.0).astype(jnp.bfloat16)


def split(value):
    high = value.astype(jnp.bfloat16)
    low = (value - high.astype(jnp.float32)).astype(jnp.bfloat16)
    return high, low


def butterfly(parts):
    step = 1
    while step < len(parts):
        parts = [
            parts[i] + parts[i + step] if i & step == 0 else parts[i - step] - parts[i]
            for i in range(len(parts))
        ]
        step *= 2
    return parts


def local_kernel(panel_ref, signs_ref, out_ref):
    signs = signs_ref[...].astype(jnp.float32)
    parts = [
        panel_ref[:, b * LANES : (b + 1) * LANES] * signs[b : b + 1, :] for b in range(BLOCKS)
    ]
    parts = butterfly(parts)
    had = hadamard(LANES, LANES)
    twice = jnp.concatenate([had, had], axis=1)
    for group in range(8):
        block = jnp.concatenate(parts[8 * group : 8 * group + 8], axis=0)
        pair = jnp.concatenate(split(block), axis=1)
        done = lax.dot_general(twice, pair, NT, preferred_element_type=jnp.float32)
        out_ref[pl.ds(group, LANES, stride=8), :] = done


def count_kernel(place_ref, samples_ref, count_ref, had_ref):
    place = place_ref[0]
    lane, top = place >> 1, place & 1
    wide_rows = 8
    count_ref[...] = jnp.zeros_like(count_ref)

    def body(step, carry):
        rows = samples_ref[pl.ds(step * wide_rows, wide_rows), :]
        owners, blocks = [], []
        for r in range(wide_rows):
            row = rows[r : r + 1, :]
            mine = jnp.logical_and((row & 127) == lane, ((row >> 12) & 1) == top)
            block = jnp.where(mine, (row >> 7) & 31, -1)
            owner = row >> 13
            owners.append(lax.broadcasted_iota(jnp.int32, (DEVICES, LANES), 0) == owner)
            blocks.append(lax.broadcasted_iota(jnp.int32, (32, LANES), 0) == block)
        hot = lambda masks: jnp.concatenate(
            [jnp.where(m, 1.0, 0.0).astype(jnp.bfloat16) for m in masks], axis=1
        )
        count_ref[...] += lax.dot_general(
            hot(blocks), hot(owners), NT, preferred_element_type=jnp.float32
        )
        return carry

    lax.fori_loop(0, SAMPLES // (wide_rows * LANES), body, 0)
    had_ref[...] = hadamard(DEVICES, DEVICES)


def across_kernel(parts_ref, count_ref, had_ref, out_ref):
    scale = 1.0 / jnp.sqrt(jnp.float32(DEVICES * LOCAL_ROWS))
    had = had_ref[...]
    columns = []
    for group in range(4):
        high, low = split(parts_ref[pl.ds(group, DEVICES, stride=4), :])
        done = jnp.dot(had, high, preferred_element_type=jnp.float32)
        done = (done + jnp.dot(had, low, preferred_element_type=jnp.float32)) * scale
        out_ref[pl.ds(group, DEVICES, stride=5), :] = done
        turned = done.T
        columns += [turned[16 * b : 16 * b + 16, :] for b in range(8)]
    counts = count_ref[...]
    weighed = [column * counts[b : b + 1, :] for b, column in enumerate(columns)]
    gram = lax.dot_general(
        jnp.concatenate(weighed, axis=1),
        jnp.concatenate(columns, axis=1),
        NT,
        precision=HIGH,
        preferred_element_type=jnp.float32,
    )
    lanes = lax.broadcasted_iota(jnp.int32, (COLUMNS, LANES), 1)
    rows = lax.broadcasted_iota(jnp.int32, (COLUMNS, LANES), 0)
    tile = jnp.where((lanes & 15) == rows, 1.0, 0.0)
    tiled = jnp.dot(gram, tile, precision=HIGH, preferred_element_type=jnp.float32)
    kept = jnp.where((lanes >> 4) == (rows & 7), tiled, 0.0)
    upper = jnp.sum(kept[:8, :], axis=0, keepdims=True)
    lower = jnp.sum(kept[8:, :], axis=0, keepdims=True)
    core = lax.broadcasted_iota(jnp.int32, (DEVICES, LANES), 0) & 1
    out_ref[pl.ds(4, DEVICES, stride=5), :] = jnp.where(
        core == 0, jnp.broadcast_to(upper, core.shape), jnp.broadcast_to(lower, core.shape)
    )


def gather_kernel(parts_ref, gram_ref):
    rows = parts_ref[pl.ds(4, DEVICES, stride=5), :]
    gram_ref[...] = jnp.sum(rows, axis=0, keepdims=True)


def place_kernel(parts_ref, out_ref):
    for top in range(2):
        for group in range(4):
            turned = parts_ref[pl.ds(top * 5 + group, LANES, stride=10), :].T
            for b in range(8):
                block = top * 32 + group * 8 + b
                out_ref[:, block * LANES : (block + 1) * LANES] = turned[16 * b : 16 * b + 16, :]


def call(kernel, outs, operands, name, specs=None, flops=0, size=1 << 20):
    return pl.pallas_call(
        kernel,
        out_shape=outs,
        in_specs=specs or [VMEM] * len(operands),
        out_specs=jax.tree.map(lambda _: VMEM, outs),
        compiler_params=pltpu.CompilerParams(vmem_limit_bytes=LIMIT),
        cost_estimate=pl.CostEstimate(flops=flops, bytes_accessed=size, transcendentals=0),
        name=name,
    )(*operands)


def per_device(panel, signs, samples):
    shape = jax.ShapeDtypeStruct
    f32 = jnp.float32
    narrow_count = lax.axis_size("narrow")
    place = lax.axis_index("wide") * narrow_count + lax.axis_index("narrow")
    parts = call(
        local_kernel,
        shape((1024, LANES), f32),
        (panel, signs.reshape(BLOCKS, LANES)),
        "local_transform",
    )
    arrived = lax.all_to_all(parts.reshape(DEVICES, 4, LANES), BOTH, 0, 0, tiled=True)
    counts, had = call(
        count_kernel,
        (shape((32, DEVICES), f32), shape((DEVICES, DEVICES), jnp.bfloat16)),
        (place.reshape(1).astype(jnp.int32), samples.reshape(LANES, LANES)),
        "count_samples",
        specs=[SMEM, VMEM],
        flops=1 << 30,
    )
    mixed_parts = call(
        across_kernel,
        shape((DEVICES * 5, LANES), f32),
        (arrived.reshape(1024, LANES), counts, had),
        "across_devices",
    )
    back = lax.all_to_all(mixed_parts.reshape(DEVICES, 1, 5 * LANES), BOTH, 0, 0, tiled=True)
    back = back.reshape(DEVICES * 5, LANES)
    half = call(gather_kernel, shape((1, LANES), f32), (back,), "sum_gram")
    other = lax.ppermute(half, "narrow", [(s, s ^ 1) for s in range(narrow_count)])
    mixed = call(place_kernel, shape((COLUMNS, LOCAL_ROWS), f32), (back,), "place_rows")
    even = place & 1 == 0
    upper = jnp.where(even, half, other).reshape(8, COLUMNS)
    lower = jnp.where(even, other, half).reshape(8, COLUMNS)
    gram = jnp.concatenate([upper, lower], axis=0) / jnp.float32(SAMPLES)
    return (mixed, gram)


def solution(mesh):
    placed = (P(None, BOTH), P(BOTH), P())
    return jax.shard_map(
        per_device,
        mesh=mesh,
        in_specs=placed,
        out_specs=(P(None, BOTH), P()),
        check_vma=False,
    )
```

```python
import jax
import jax.numpy as jnp
from jax import lax
from jax.experimental import pallas as pl
from jax.experimental.pallas import tpu as pltpu
from jax.sharding import Mesh
from jax.sharding import PartitionSpec as P

COLUMNS = 16
LANES = 128
BLOCKS = 64
CHIPS = 128
LOCAL_ROWS = BLOCKS * LANES
ROWS = 2 * CHIPS * LOCAL_ROWS
SAMPLES = 16384
WIDTH = 10
CHIP_AXES = ("wide", "slow")
ALL_AXES = ("wide", "slow", "core")
NT = (((1,), (1,)), ((), ()))
HIGH = lax.Precision.HIGHEST
VMEM = pl.BlockSpec(memory_space=pltpu.VMEM)
SMEM = pl.BlockSpec(memory_space=pltpu.SMEM)
HBM = pl.BlockSpec(memory_space=pltpu.HBM)
LIMIT = 32 * 1024 * 1024


def hadamard_twice():
    first = lax.broadcasted_iota(jnp.int32, (LANES, LANES), 0)
    second = lax.broadcasted_iota(jnp.int32, (LANES, LANES), 1)
    bits = first & second
    bits = bits ^ (bits >> 4)
    bits = bits ^ (bits >> 2)
    bits = bits ^ (bits >> 1)
    had = jnp.where((bits & 1) == 0, 1.0, -1.0).astype(jnp.bfloat16)
    return jnp.concatenate([had, had], axis=1)


def split(value):
    high = value.astype(jnp.bfloat16)
    low = (value - high.astype(jnp.float32)).astype(jnp.bfloat16)
    return high, low


def butterfly(parts):
    step = 1
    while step < len(parts):
        parts = [
            parts[i] + parts[i + step] if i & step == 0 else parts[i - step] - parts[i]
            for i in range(len(parts))
        ]
        step *= 2
    return parts


def local_kernel(panel_hbm, signs_hbm, out_ref, panel_ref, signs_ref, panel_sem, signs_sem):
    halves = [
        pltpu.make_async_copy(
            panel_hbm.at[pl.ds(8 * half, 8), :], panel_ref.at[half], panel_sem.at[half]
        )
        for half in range(2)
    ]
    signs_copy = pltpu.make_async_copy(signs_hbm, signs_ref, signs_sem)
    signs_copy.start()
    for half in halves:
        half.start()
    twice = hadamard_twice()
    signs_copy.wait()
    for half in range(2):
        halves[half].wait()
        signs = signs_ref[...].astype(jnp.float32)
        parts = [
            panel_ref[half, :, b * LANES : (b + 1) * LANES] * signs[b : b + 1, :]
            for b in range(BLOCKS)
        ]
        parts = butterfly(parts)
        for quarter in range(4):
            block = jnp.concatenate(parts[16 * quarter : 16 * quarter + 16], axis=0)
            pair = jnp.concatenate(split(block), axis=1)
            done = lax.dot_general(twice, pair, NT, preferred_element_type=jnp.float32)
            out_ref[pl.ds(4 * half + quarter, LANES, stride=8), :] = done


def count_kernel(chip_ref, samples_ref, count_ref):
    chip = chip_ref[0]
    wide_rows = 8
    count_ref[...] = jnp.zeros_like(count_ref)

    def body(step, carry):
        rows = samples_ref[pl.ds(step * wide_rows, wide_rows), :]
        owners, places = [], []
        for r in range(wide_rows):
            row = rows[r : r + 1, :]
            place = ((row >> 13) & 1) * BLOCKS + ((row >> 7) & 63)
            place = jnp.where((row & 127) == chip, place, -1)
            owner = row >> 14
            index = lax.broadcasted_iota(jnp.int32, (CHIPS, LANES), 0)
            owners.append(jnp.where(index == owner, 1.0, 0.0).astype(jnp.bfloat16))
            places.append(jnp.where(index == place, 1.0, 0.0).astype(jnp.bfloat16))
        count_ref[...] += lax.dot_general(
            jnp.concatenate(places, axis=1),
            jnp.concatenate(owners, axis=1),
            NT,
            preferred_element_type=jnp.float32,
        )
        return carry

    lax.fori_loop(0, SAMPLES // (wide_rows * LANES), body, 0)


def chips_transform(parts_ref, group, twice):
    pair = jnp.concatenate(split(parts_ref[pl.ds(group, CHIPS, stride=8), :]), axis=0)
    return jnp.dot(twice, pair, preferred_element_type=jnp.float32)


def own_kernel(parts_ref, out_ref, turned_ref):
    twice = hadamard_twice()
    for group in range(8):
        done = chips_transform(parts_ref, group, twice)
        rows = slice(group * CHIPS, (group + 1) * CHIPS)
        out_ref[rows, :] = done
        turned_ref[rows, :] = done.T


def both_kernel(core_ref, parts_ref, own_ref, turned_ref, count_ref, out_ref):
    scale = 1.0 / jnp.sqrt(jnp.float32(ROWS))
    side = (1 - 2 * core_ref[0]).astype(jnp.float32) * scale
    twice = hadamard_twice()
    sums, gaps = [], []
    for group in range(8):
        done = chips_transform(parts_ref, group, twice)
        rows = slice(group * CHIPS, (group + 1) * CHIPS)
        out_ref[pl.ds(group, CHIPS, stride=WIDTH), :] = done * scale + own_ref[rows, :] * side
        other, own = done.T, turned_ref[rows, :]
        sums.append((own + other) * scale)
        gaps.append((own - other) * scale)
    columns = []
    for turned in (sums, gaps):
        for b in range(BLOCKS):
            rows = slice(8 * (b % 16), 8 * (b % 16) + 8)
            columns.append(
                jnp.concatenate([turned[b // 16][rows, :], turned[4 + b // 16][rows, :]], axis=0)
            )
    counts = count_ref[...]
    weighed = [column * counts[b : b + 1, :] for b, column in enumerate(columns)]
    weighed = jnp.concatenate(split(jnp.concatenate(weighed, axis=1)), axis=0)
    columns = jnp.concatenate(split(jnp.concatenate(columns, axis=1)), axis=0)
    gram = lax.dot_general(weighed, columns, NT, preferred_element_type=jnp.float32)
    gram = gram[:, :COLUMNS] + gram[:, COLUMNS:]
    gram = gram[:COLUMNS, :] + gram[COLUMNS:, :]
    lanes = lax.broadcasted_iota(jnp.int32, (COLUMNS, LANES), 1)
    rows = lax.broadcasted_iota(jnp.int32, (COLUMNS, LANES), 0)
    tile = jnp.where((lanes & 15) == rows, 1.0, 0.0)
    tiled = jnp.dot(gram, tile, precision=HIGH, preferred_element_type=jnp.float32)
    kept = jnp.where((lanes >> 4) == (rows & 7), tiled, 0.0)
    for half in range(2):
        flat = jnp.sum(kept[8 * half : 8 * half + 8, :], axis=0, keepdims=True)
        out_ref[pl.ds(8 + half, CHIPS, stride=WIDTH), :] = jnp.broadcast_to(flat, (CHIPS, LANES))


def place_kernel(parts_ref, out_ref, gram_ref):
    for half in range(2):
        for quarter in range(4):
            turned = parts_ref[pl.ds(4 * half + quarter, LANES, stride=WIDTH), :].T
            for b in range(16):
                block = quarter * 16 + b
                out_ref[8 * half : 8 * half + 8, block * LANES : (block + 1) * LANES] = turned[
                    8 * b : 8 * b + 8, :
                ]
    lanes = lax.broadcasted_iota(jnp.int32, (8, LANES), 1)
    rows = lax.broadcasted_iota(jnp.int32, (8, LANES), 0)
    pick = jnp.where(
        (lax.broadcasted_iota(jnp.int32, (LANES, COLUMNS), 0) & 15)
        == lax.broadcasted_iota(jnp.int32, (LANES, COLUMNS), 1),
        1.0,
        0.0,
    )
    for half in range(2):
        flat = jnp.sum(
            parts_ref[pl.ds(8 + half, CHIPS, stride=WIDTH), :], axis=0, keepdims=True
        )
        spread = jnp.where((lanes >> 4) == rows, jnp.broadcast_to(flat, (8, LANES)), 0.0)
        block = jnp.dot(spread, pick, precision=HIGH, preferred_element_type=jnp.float32)
        gram_ref[8 * half : 8 * half + 8, :] = block / jnp.float32(SAMPLES)


def call(kernel, outs, operands, name, specs=None, scratch=(), flops=0, limit=LIMIT):
    return pl.pallas_call(
        kernel,
        out_shape=outs,
        in_specs=specs or [VMEM] * len(operands),
        out_specs=jax.tree.map(lambda _: VMEM, outs),
        scratch_shapes=scratch,
        compiler_params=pltpu.CompilerParams(vmem_limit_bytes=limit),
        cost_estimate=pl.CostEstimate(flops=flops, bytes_accessed=1 << 20, transcendentals=0),
        name=name,
    )(*operands)


def per_device(panel, signs, samples):
    f32 = jnp.float32
    whole = jax.ShapeDtypeStruct((1024, LANES), f32)
    core = lax.axis_index("core").astype(jnp.int32).reshape(1)
    chip = lax.axis_index("wide") * lax.axis_size("slow") + lax.axis_index("slow")
    chip = chip.astype(jnp.int32).reshape(1)
    exchange = lambda value: lax.all_to_all(value, CHIP_AXES, 0, 0, tiled=True)
    parts = call(
        local_kernel,
        whole,
        (panel, signs.reshape(BLOCKS, LANES)),
        "local_transform",
        specs=[HBM, HBM],
        scratch=[
            pltpu.VMEM((2, 8, LOCAL_ROWS), f32),
            pltpu.VMEM((BLOCKS, LANES), jnp.int32),
            pltpu.SemaphoreType.DMA((2,)),
            pltpu.SemaphoreType.DMA(()),
        ],
        limit=60 * 1024 * 1024,
    )
    parts = exchange(parts.reshape(CHIPS, 8, LANES)).reshape(1024, LANES)
    counts = call(
        count_kernel,
        jax.ShapeDtypeStruct((2 * BLOCKS, CHIPS), f32),
        (chip, samples.reshape(LANES, LANES)),
        "count_samples",
        specs=[SMEM, VMEM],
        flops=1 << 30,
    )
    parts, counts = lax.optimization_barrier((parts, counts))
    other = lax.ppermute(parts, "core", [(0, 1), (1, 0)])
    own, turned = call(own_kernel, (whole, whole), (parts,), "own_chips_transform", flops=1 << 28)
    back = call(
        both_kernel,
        jax.ShapeDtypeStruct((CHIPS * WIDTH, LANES), f32),
        (core, other, own, turned, counts),
        "both_cores",
        specs=[SMEM] + [VMEM] * 4,
    )
    back = exchange(back.reshape(CHIPS, 1, WIDTH * LANES)).reshape(CHIPS * WIDTH, LANES)
    return call(
        place_kernel,
        (
            jax.ShapeDtypeStruct((COLUMNS, LOCAL_ROWS), f32),
            jax.ShapeDtypeStruct((COLUMNS, COLUMNS), f32),
        ),
        (back,),
        "place_rows",
    )


def solution(mesh):
    wide, narrow = mesh.devices.shape
    split_mesh = Mesh(mesh.devices.reshape(wide, narrow // 2, 2), ALL_AXES)
    return jax.shard_map(
        per_device,
        mesh=split_mesh,
        in_specs=(P(None, ALL_AXES), P(ALL_AXES), P()),
        out_specs=(P(None, ALL_AXES), P()),
        check_vma=False,
    )
```

```python
import jax
import jax.numpy as jnp
from jax import lax
from jax.experimental import pallas as pl
from jax.experimental.pallas import tpu as pltpu
from jax.sharding import Mesh
from jax.sharding import PartitionSpec as P

COLUMNS = 16
LANES = 128
BLOCKS = 64
CHIPS = 128
LOCAL_ROWS = BLOCKS * LANES
ROWS = 2 * CHIPS * LOCAL_ROWS
SAMPLES = 16384
WIDTH = 10
CHIP_AXES = ("wide", "slow")
ALL_AXES = ("wide", "slow", "core")
NT = (((1,), (1,)), ((), ()))
HIGH = lax.Precision.HIGHEST
VMEM = pl.BlockSpec(memory_space=pltpu.VMEM)
HBM = pl.BlockSpec(memory_space=pltpu.HBM)
LIMIT = 32 * 1024 * 1024


def hadamard_twice():
    first = lax.broadcasted_iota(jnp.int32, (LANES, LANES), 0)
    second = lax.broadcasted_iota(jnp.int32, (LANES, LANES), 1)
    bits = first & second
    bits = bits ^ (bits >> 4)
    bits = bits ^ (bits >> 2)
    bits = bits ^ (bits >> 1)
    had = jnp.where((bits & 1) == 0, 1.0, -1.0).astype(jnp.bfloat16)
    return jnp.concatenate([had, had], axis=1)


def split(value):
    high = value.astype(jnp.bfloat16)
    low = (value - high.astype(jnp.float32)).astype(jnp.bfloat16)
    return high, low


def butterfly(parts):
    step = 1
    while step < len(parts):
        parts = [
            parts[i] + parts[i + step] if i & step == 0 else parts[i - step] - parts[i]
            for i in range(len(parts))
        ]
        step *= 2
    return parts


def bring_kernel(panel_hbm, panel_ref, sem):
    copy = pltpu.make_async_copy(panel_hbm, panel_ref, sem)
    copy.start()
    copy.wait()


def local_kernel(panel_ref, signs_ref, out_ref):
    twice = hadamard_twice()
    signs = signs_ref[...].astype(jnp.float32)
    for half in range(2):
        parts = [
            panel_ref[8 * half : 8 * half + 8, b * LANES : (b + 1) * LANES] * signs[b : b + 1, :]
            for b in range(BLOCKS)
        ]
        parts = butterfly(parts)
        for quarter in range(4):
            block = jnp.concatenate(parts[16 * quarter : 16 * quarter + 16], axis=0)
            pair = jnp.concatenate(split(block), axis=1)
            done = lax.dot_general(twice, pair, NT, preferred_element_type=jnp.float32)
            out_ref[pl.ds(4 * half + quarter, LANES, stride=8), :] = done


def count_kernel(samples_ref, count_ref):
    chip = lax.axis_index("wide") * lax.axis_size("slow") + lax.axis_index("slow")
    rows = samples_ref[...]
    place = ((rows >> 13) & 1) * BLOCKS + ((rows >> 7) & 63)
    place = jnp.where((rows & 127) == chip, place, -1).astype(jnp.float32)
    owner = (rows >> 14).astype(jnp.float32)
    index = lax.broadcasted_iota(jnp.int32, (CHIPS, LANES), 0)
    index = index.astype(jnp.float32).astype(jnp.bfloat16)
    one, zero = jnp.ones_like(index), jnp.zeros_like(index)

    def hot(values):
        spread = [
            jnp.broadcast_to(values[r : r + 1, :], index.shape).astype(jnp.bfloat16)
            for r in range(SAMPLES // LANES)
        ]
        return jnp.concatenate([jnp.where(index == row, one, zero) for row in spread], axis=1)

    count_ref[...] = lax.dot_general(
        hot(place), hot(owner), NT, preferred_element_type=jnp.float32
    )


def chips_transform(parts_ref, group, twice):
    pair = jnp.concatenate(split(parts_ref[pl.ds(group, CHIPS, stride=8), :]), axis=0)
    return jnp.dot(twice, pair, preferred_element_type=jnp.float32)


def own_kernel(parts_ref, out_ref, turned_ref):
    scale = 1.0 / jnp.sqrt(jnp.float32(ROWS))
    twice = hadamard_twice()
    for group in range(8):
        done = chips_transform(parts_ref, group, twice)
        rows = slice(group * CHIPS, (group + 1) * CHIPS)
        done = done * scale
        out_ref[rows, :] = done
        turned_ref[rows, :] = done.T


def both_kernel(parts_ref, own_ref, turned_ref, count_ref, out_ref):
    scale = 1.0 / jnp.sqrt(jnp.float32(ROWS))
    side = (1 - 2 * lax.axis_index("core")).astype(jnp.float32)
    twice = hadamard_twice()
    sums, gaps = [], []
    for group in range(8):
        done = chips_transform(parts_ref, group, twice) * scale
        rows = slice(group * CHIPS, (group + 1) * CHIPS)
        out_ref[pl.ds(group, CHIPS, stride=WIDTH), :] = done + own_ref[rows, :] * side
        other, own = done.T, turned_ref[rows, :]
        sums.append(own + other)
        gaps.append(own - other)
    columns = []
    for turned in (sums, gaps):
        for b in range(BLOCKS):
            rows = slice(8 * (b % 16), 8 * (b % 16) + 8)
            columns.append(
                jnp.concatenate([turned[b // 16][rows, :], turned[4 + b // 16][rows, :]], axis=0)
            )
    counts = count_ref[...]
    weighed = [column * counts[b : b + 1, :] for b, column in enumerate(columns)]
    weighed = jnp.concatenate(split(jnp.concatenate(weighed, axis=1)), axis=0)
    columns = jnp.concatenate(split(jnp.concatenate(columns, axis=1)), axis=0)
    gram = lax.dot_general(weighed, columns, NT, preferred_element_type=jnp.float32)
    gram = gram[:, :COLUMNS] + gram[:, COLUMNS:]
    gram = gram[:COLUMNS, :] + gram[COLUMNS:, :]
    lanes = lax.broadcasted_iota(jnp.int32, (COLUMNS, LANES), 1)
    rows = lax.broadcasted_iota(jnp.int32, (COLUMNS, LANES), 0)
    tile = jnp.where((lanes & 15) == rows, 1.0, 0.0)
    tiled = jnp.dot(gram, tile, precision=HIGH, preferred_element_type=jnp.float32)
    kept = jnp.where((lanes >> 4) == (rows & 7), tiled, 0.0)
    for half in range(2):
        flat = jnp.sum(kept[8 * half : 8 * half + 8, :], axis=0, keepdims=True)
        out_ref[pl.ds(8 + half, CHIPS, stride=WIDTH), :] = jnp.broadcast_to(flat, (CHIPS, LANES))


def place_kernel(parts_ref, out_ref, gram_ref):
    for half in range(2):
        for quarter in range(4):
            turned = parts_ref[pl.ds(4 * half + quarter, LANES, stride=WIDTH), :].T
            for b in range(16):
                block = quarter * 16 + b
                out_ref[8 * half : 8 * half + 8, block * LANES : (block + 1) * LANES] = turned[
                    8 * b : 8 * b + 8, :
                ]
    lanes = lax.broadcasted_iota(jnp.int32, (8, LANES), 1)
    rows = lax.broadcasted_iota(jnp.int32, (8, LANES), 0)
    pick = jnp.where(
        (lax.broadcasted_iota(jnp.int32, (LANES, COLUMNS), 0) & 15)
        == lax.broadcasted_iota(jnp.int32, (LANES, COLUMNS), 1),
        1.0,
        0.0,
    )
    for half in range(2):
        flat = jnp.sum(
            parts_ref[pl.ds(8 + half, CHIPS, stride=WIDTH), :], axis=0, keepdims=True
        )
        spread = jnp.where((lanes >> 4) == rows, jnp.broadcast_to(flat, (8, LANES)), 0.0)
        block = jnp.dot(spread, pick, precision=HIGH, preferred_element_type=jnp.float32)
        gram_ref[8 * half : 8 * half + 8, :] = block / jnp.float32(SAMPLES)


def call(kernel, outs, operands, name, specs=None, scratch=(), flops=0, limit=LIMIT):
    return pl.pallas_call(
        kernel,
        out_shape=outs,
        in_specs=specs or [VMEM] * len(operands),
        out_specs=jax.tree.map(lambda _: VMEM, outs),
        scratch_shapes=scratch,
        compiler_params=pltpu.CompilerParams(vmem_limit_bytes=limit),
        cost_estimate=pl.CostEstimate(flops=flops, bytes_accessed=1 << 20, transcendentals=0),
        name=name,
    )(*operands)


def per_device(panel, signs, samples):
    f32 = jnp.float32
    whole = jax.ShapeDtypeStruct((1024, LANES), f32)
    exchange = lambda value: lax.all_to_all(value, CHIP_AXES, 0, 0, tiled=True)
    panel = call(
        bring_kernel,
        jax.ShapeDtypeStruct((COLUMNS, LOCAL_ROWS), f32),
        (panel,),
        "bring_panel",
        specs=[HBM],
        scratch=[pltpu.SemaphoreType.DMA(())],
        limit=53 * 1024 * 1024,
    )
    parts = call(local_kernel, whole, (panel, signs.reshape(BLOCKS, LANES)), "local_transform")
    parts = exchange(parts.reshape(CHIPS, 8, LANES)).reshape(1024, LANES)
    parts, samples = lax.optimization_barrier((parts, samples))
    other = lax.ppermute(parts, "core", [(0, 1), (1, 0)])
    own, turned = call(own_kernel, (whole, whole), (parts,), "own_chips_transform", flops=1 << 28)
    counts = call(
        count_kernel,
        jax.ShapeDtypeStruct((2 * BLOCKS, CHIPS), f32),
        (samples.reshape(LANES, LANES),),
        "count_samples",
        flops=1 << 30,
    )
    back = call(
        both_kernel,
        jax.ShapeDtypeStruct((CHIPS * WIDTH, LANES), f32),
        (other, own, turned, counts),
        "both_cores",
    )
    back = exchange(back.reshape(CHIPS, 1, WIDTH * LANES)).reshape(CHIPS * WIDTH, LANES)
    return call(
        place_kernel,
        (
            jax.ShapeDtypeStruct((COLUMNS, LOCAL_ROWS), f32),
            jax.ShapeDtypeStruct((COLUMNS, COLUMNS), f32),
        ),
        (back,),
        "place_rows",
    )


def solution(mesh):
    wide, narrow = mesh.devices.shape
    split_mesh = Mesh(mesh.devices.reshape(wide, narrow // 2, 2), ALL_AXES)
    return jax.shard_map(
        per_device,
        mesh=split_mesh,
        in_specs=(P(None, ALL_AXES), P(ALL_AXES), P()),
        out_specs=(P(None, ALL_AXES), P()),
        check_vma=False,
    )
```

```python
import jax
import jax.numpy as jnp
from jax import lax
from jax.experimental import pallas as pl
from jax.experimental.pallas import tpu as pltpu
from jax.sharding import Mesh
from jax.sharding import PartitionSpec as P

COLUMNS = 16
LANES = 128
BLOCKS = 64
CHIPS = 128
LOCAL_ROWS = BLOCKS * LANES
ROWS = 2 * CHIPS * LOCAL_ROWS
SAMPLES = 16384
WIDTH = 10
CHIP_AXES = ("wide", "slow")
ALL_AXES = ("wide", "slow", "core")
NT = (((1,), (1,)), ((), ()))
HIGH = lax.Precision.HIGHEST
VMEM = pl.BlockSpec(memory_space=pltpu.VMEM)
HBM = pl.BlockSpec(memory_space=pltpu.HBM)
LIMIT = 32 * 1024 * 1024


def hadamard_twice():
    first = lax.broadcasted_iota(jnp.int32, (LANES, LANES), 0)
    second = lax.broadcasted_iota(jnp.int32, (LANES, LANES), 1)
    bits = first & second
    bits = bits ^ (bits >> 4)
    bits = bits ^ (bits >> 2)
    bits = bits ^ (bits >> 1)
    had = jnp.where((bits & 1) == 0, 1.0, -1.0).astype(jnp.bfloat16)
    return jnp.concatenate([had, had], axis=1)


def split(value):
    high = value.astype(jnp.bfloat16)
    low = (value - high.astype(jnp.float32)).astype(jnp.bfloat16)
    return high, low


def butterfly(parts):
    step = 1
    while step < len(parts):
        parts = [
            parts[i] + parts[i + step] if i & step == 0 else parts[i - step] - parts[i]
            for i in range(len(parts))
        ]
        step *= 2
    return parts


def local_kernel(
    panel_hbm, signs_hbm, samples_hbm, out_ref, samples_ref, panel_ref, signs_ref, sems
):
    signs_copy = pltpu.make_async_copy(signs_hbm, signs_ref, sems.at[2])
    signs_copy.start()
    halves = []
    for half in range(2):
        halves.append(
            pltpu.make_async_copy(
                panel_hbm.at[pl.ds(8 * half, 8), :], panel_ref.at[half], sems.at[half]
            )
        )
        halves[half].start()
    samples_copy = pltpu.make_async_copy(samples_hbm, samples_ref, sems.at[3])
    samples_copy.start()
    twice = hadamard_twice()
    signs_copy.wait()
    for half in range(2):
        halves[half].wait()
        signs = signs_ref[...].astype(jnp.float32)
        parts = [
            panel_ref[half, :, b * LANES : (b + 1) * LANES] * signs[b : b + 1, :]
            for b in range(BLOCKS)
        ]
        parts = butterfly(parts)
        for quarter in range(4):
            block = jnp.concatenate(parts[16 * quarter : 16 * quarter + 16], axis=0)
            pair = jnp.concatenate(split(block), axis=1)
            done = lax.dot_general(twice, pair, NT, preferred_element_type=jnp.float32)
            out_ref[pl.ds(4 * half + quarter, LANES, stride=8), :] = done
    samples_copy.wait()


def count_kernel(samples_ref, count_ref):
    chip = lax.axis_index("wide") * lax.axis_size("slow") + lax.axis_index("slow")
    rows = samples_ref[...]
    place = ((rows >> 13) & 1) * BLOCKS + ((rows >> 7) & 63)
    place = jnp.where((rows & 127) == chip, place, -1).astype(jnp.float32)
    owner = (rows >> 14).astype(jnp.float32)
    index = lax.broadcasted_iota(jnp.int32, (CHIPS, LANES), 0)
    index = index.astype(jnp.float32).astype(jnp.bfloat16)
    one, zero = jnp.ones_like(index), jnp.zeros_like(index)

    def hot(values):
        spread = [
            jnp.broadcast_to(values[r : r + 1, :], index.shape).astype(jnp.bfloat16)
            for r in range(SAMPLES // LANES)
        ]
        return jnp.concatenate([jnp.where(index == row, one, zero) for row in spread], axis=1)

    count_ref[...] = lax.dot_general(
        hot(place), hot(owner), NT, preferred_element_type=jnp.float32
    )


def chips_transform(parts_ref, group, twice):
    pair = jnp.concatenate(split(parts_ref[pl.ds(group, CHIPS, stride=8), :]), axis=0)
    return jnp.dot(twice, pair, preferred_element_type=jnp.float32)


def own_kernel(parts_ref, out_ref, turned_ref):
    scale = 1.0 / jnp.sqrt(jnp.float32(ROWS))
    twice = hadamard_twice()
    for group in range(8):
        done = chips_transform(parts_ref, group, twice)
        rows = slice(group * CHIPS, (group + 1) * CHIPS)
        done = done * scale
        out_ref[rows, :] = done
        turned_ref[rows, :] = done.T


def both_kernel(parts_ref, own_ref, turned_ref, count_ref, out_ref):
    scale = 1.0 / jnp.sqrt(jnp.float32(ROWS))
    side = (1 - 2 * lax.axis_index("core")).astype(jnp.float32)
    twice = hadamard_twice()
    sums, gaps = [], []
    for group in range(8):
        done = chips_transform(parts_ref, group, twice) * scale
        rows = slice(group * CHIPS, (group + 1) * CHIPS)
        out_ref[pl.ds(group, CHIPS, stride=WIDTH), :] = done + own_ref[rows, :] * side
        other, own = done.T, turned_ref[rows, :]
        sums.append(own + other)
        gaps.append(own - other)
    columns = []
    for turned in (sums, gaps):
        for b in range(BLOCKS):
            rows = slice(8 * (b % 16), 8 * (b % 16) + 8)
            columns.append(
                jnp.concatenate([turned[b // 16][rows, :], turned[4 + b // 16][rows, :]], axis=0)
            )
    counts = count_ref[...]
    weighed = [column * counts[b : b + 1, :] for b, column in enumerate(columns)]
    weighed = jnp.concatenate(split(jnp.concatenate(weighed, axis=1)), axis=0)
    columns = jnp.concatenate(split(jnp.concatenate(columns, axis=1)), axis=0)
    gram = lax.dot_general(weighed, columns, NT, preferred_element_type=jnp.float32)
    gram = gram[:, :COLUMNS] + gram[:, COLUMNS:]
    gram = gram[:COLUMNS, :] + gram[COLUMNS:, :]
    lanes = lax.broadcasted_iota(jnp.int32, (COLUMNS, LANES), 1)
    rows = lax.broadcasted_iota(jnp.int32, (COLUMNS, LANES), 0)
    tile = jnp.where((lanes & 15) == rows, 1.0, 0.0)
    tiled = jnp.dot(gram, tile, precision=HIGH, preferred_element_type=jnp.float32)
    kept = jnp.where((lanes >> 4) == (rows & 7), tiled, 0.0)
    for half in range(2):
        flat = jnp.sum(kept[8 * half : 8 * half + 8, :], axis=0, keepdims=True)
        out_ref[pl.ds(8 + half, CHIPS, stride=WIDTH), :] = jnp.broadcast_to(flat, (CHIPS, LANES))


def place_kernel(parts_ref, out_hbm, gram_hbm, out_ref, gram_ref, sems):
    lanes = lax.broadcasted_iota(jnp.int32, (8, LANES), 1)
    rows = lax.broadcasted_iota(jnp.int32, (8, LANES), 0)
    pick = jnp.where(
        (lax.broadcasted_iota(jnp.int32, (LANES, COLUMNS), 0) & 15)
        == lax.broadcasted_iota(jnp.int32, (LANES, COLUMNS), 1),
        1.0,
        0.0,
    )
    copies = []
    for half in range(2):
        for quarter in range(4):
            turned = parts_ref[pl.ds(4 * half + quarter, LANES, stride=WIDTH), :].T
            for b in range(16):
                block = quarter * 16 + b
                out_ref[half, :, block * LANES : (block + 1) * LANES] = turned[
                    8 * b : 8 * b + 8, :
                ]
        copies.append(
            pltpu.make_async_copy(
                out_ref.at[half], out_hbm.at[pl.ds(8 * half, 8), :], sems.at[half]
            )
        )
        copies[half].start()
        flat = jnp.sum(
            parts_ref[pl.ds(8 + half, CHIPS, stride=WIDTH), :], axis=0, keepdims=True
        )
        spread = jnp.where((lanes >> 4) == rows, jnp.broadcast_to(flat, (8, LANES)), 0.0)
        block = jnp.dot(spread, pick, precision=HIGH, preferred_element_type=jnp.float32)
        gram_ref[8 * half : 8 * half + 8, :] = block / jnp.float32(SAMPLES)
    copies.append(pltpu.make_async_copy(gram_ref, gram_hbm, sems.at[2]))
    copies[2].start()
    for copy in copies:
        copy.wait()


def call(kernel, outs, operands, name, specs=None, out_specs=None, scratch=(), flops=0, limit=LIMIT):
    return pl.pallas_call(
        kernel,
        out_shape=outs,
        in_specs=specs or [VMEM] * len(operands),
        out_specs=out_specs or jax.tree.map(lambda _: VMEM, outs),
        scratch_shapes=scratch,
        compiler_params=pltpu.CompilerParams(vmem_limit_bytes=limit),
        cost_estimate=pl.CostEstimate(flops=flops, bytes_accessed=1 << 20, transcendentals=0),
        name=name,
    )(*operands)


def per_device(panel, signs, samples):
    f32 = jnp.float32
    whole = jax.ShapeDtypeStruct((1024, LANES), f32)
    exchange = lambda value: lax.all_to_all(value, CHIP_AXES, 0, 0, tiled=True)
    in_hbm = lambda value: pltpu.with_memory_space_constraint(value, pltpu.HBM)
    parts, samples = call(
        local_kernel,
        (pltpu.VMEM((1024, LANES), f32), pltpu.VMEM((LANES, LANES), jnp.int32)),
        (
            in_hbm(panel),
            in_hbm(signs.reshape(BLOCKS, LANES)),
            in_hbm(samples.reshape(LANES, LANES)),
        ),
        "local_transform",
        specs=[HBM] * 3,
        scratch=[
            pltpu.VMEM((2, 8, LOCAL_ROWS), f32),
            pltpu.VMEM((BLOCKS, LANES), jnp.int32),
            pltpu.SemaphoreType.DMA((4,)),
        ],
    )
    parts = exchange(parts.reshape(CHIPS, 8, LANES)).reshape(1024, LANES)
    parts, samples = lax.optimization_barrier((parts, samples))
    other = lax.ppermute(parts, "core", [(0, 1), (1, 0)])
    own, turned = call(own_kernel, (whole, whole), (parts,), "own_chips_transform", flops=1 << 28)
    counts = call(
        count_kernel,
        jax.ShapeDtypeStruct((2 * BLOCKS, CHIPS), f32),
        (samples,),
        "count_samples",
        flops=1 << 30,
    )
    back = call(
        both_kernel,
        jax.ShapeDtypeStruct((CHIPS * WIDTH, LANES), f32),
        (other, own, turned, counts),
        "both_cores",
    )
    back = exchange(back.reshape(CHIPS, 1, WIDTH * LANES)).reshape(CHIPS * WIDTH, LANES)
    return call(
        place_kernel,
        (
            jax.ShapeDtypeStruct((COLUMNS, LOCAL_ROWS), f32),
            jax.ShapeDtypeStruct((COLUMNS, COLUMNS), f32),
        ),
        (back,),
        "place_rows",
        out_specs=(HBM, HBM),
        scratch=[
            pltpu.VMEM((2, 8, LOCAL_ROWS), f32),
            pltpu.VMEM((COLUMNS, COLUMNS), f32),
            pltpu.SemaphoreType.DMA((3,)),
        ],
    )


def solution(mesh):
    wide, narrow = mesh.devices.shape
    split_mesh = Mesh(mesh.devices.reshape(wide, narrow // 2, 2), ALL_AXES)
    return jax.shard_map(
        per_device,
        mesh=split_mesh,
        in_specs=(P(None, ALL_AXES), P(ALL_AXES), P()),
        out_specs=(P(None, ALL_AXES), P()),
        check_vma=False,
    )
```

```python
import jax
import jax.numpy as jnp
from jax import lax
from jax.experimental import pallas as pl
from jax.experimental.pallas import tpu as pltpu
from jax.sharding import Mesh
from jax.sharding import PartitionSpec as P

COLUMNS = 16
LANES = 128
BLOCKS = 64
CHIPS = 128
LOCAL_ROWS = BLOCKS * LANES
ROWS = 2 * CHIPS * LOCAL_ROWS
SAMPLES = 16384
CHUNKS = 8
WIDTH = 10
CHIP_AXES = ("wide", "slow")
ALL_AXES = ("wide", "slow", "core")
NT = (((1,), (1,)), ((), ()))
VMEM = pl.BlockSpec(memory_space=pltpu.VMEM)
HBM = pl.BlockSpec(memory_space=pltpu.HBM)
LIMIT = 32 * 1024 * 1024


def hadamard_twice():
    first = lax.broadcasted_iota(jnp.int32, (LANES, LANES), 0)
    second = lax.broadcasted_iota(jnp.int32, (LANES, LANES), 1)
    bits = first & second
    bits = bits ^ (bits >> 4)
    bits = bits ^ (bits >> 2)
    bits = bits ^ (bits >> 1)
    had = jnp.where((bits & 1) == 0, 1.0, -1.0).astype(jnp.bfloat16)
    return jnp.concatenate([had, had], axis=1)


def split(value):
    high = value.astype(jnp.bfloat16)
    low = (value - high.astype(jnp.float32)).astype(jnp.bfloat16)
    return high, low


def columns_alike(rows, lanes):
    first = lax.broadcasted_iota(jnp.int32, (rows, lanes), 0)
    second = lax.broadcasted_iota(jnp.int32, (rows, lanes), 1)
    return jnp.where(((first ^ second) & 15) == 0, 1.0, 0.0).astype(jnp.bfloat16)


def exact_pick(value, ones):
    count = value.shape[0]
    high, low = split(value)
    rest = value - high.astype(jnp.float32) - low.astype(jnp.float32)
    parts = jnp.concatenate([high, low, rest.astype(jnp.bfloat16)], axis=0)
    done = jnp.dot(parts, ones, preferred_element_type=jnp.float32)
    return done[:count, :] + done[count : 2 * count, :] + done[2 * count :, :]


def butterfly(parts):
    step = 1
    while step < len(parts):
        parts = [
            parts[i] + parts[i + step] if i & step == 0 else parts[i - step] - parts[i]
            for i in range(len(parts))
        ]
        step *= 2
    return parts


def local_kernel(
    panel_hbm, signs_hbm, samples_hbm, out_ref, samples_ref, panel_ref, signs_ref, sems
):
    signs_copy = pltpu.make_async_copy(signs_hbm, signs_ref, sems.at[2])
    signs_copy.start()
    halves = []
    for half in range(2):
        halves.append(
            pltpu.make_async_copy(
                panel_hbm.at[pl.ds(8 * half, 8), :], panel_ref.at[half], sems.at[half]
            )
        )
        halves[half].start()
    samples_copy = pltpu.make_async_copy(samples_hbm, samples_ref, sems.at[3])
    samples_copy.start()
    twice = hadamard_twice()
    signs_copy.wait()
    for half in range(2):
        halves[half].wait()
        signs = signs_ref[...].astype(jnp.float32)
        parts = [
            panel_ref[half, :, b * LANES : (b + 1) * LANES] * signs[b : b + 1, :]
            for b in range(BLOCKS)
        ]
        parts = butterfly(parts)
        for quarter in range(4):
            block = jnp.concatenate(parts[16 * quarter : 16 * quarter + 16], axis=0)
            pair = jnp.concatenate(split(block), axis=1)
            done = lax.dot_general(twice, pair, NT, preferred_element_type=jnp.float32)
            out_ref[pl.ds(4 * half + quarter, LANES, stride=8), :] = done
    samples_copy.wait()


def count_kernel(samples_ref, count_ref):
    chip = lax.axis_index("wide") * lax.axis_size("slow") + lax.axis_index("slow")
    rows = samples_ref[...]
    place = ((rows >> 13) & 1) * BLOCKS + ((rows >> 7) & 63)
    place = jnp.where((rows & 127) == chip, place, -1).astype(jnp.float32)
    owner = (rows >> 14).astype(jnp.float32)
    index = lax.broadcasted_iota(jnp.int32, (CHIPS, LANES), 0)
    index = index.astype(jnp.float32).astype(jnp.bfloat16)
    one, zero = jnp.ones_like(index), jnp.zeros_like(index)

    def hot(values):
        spread = [
            jnp.broadcast_to(values[r : r + 1, :], index.shape).astype(jnp.bfloat16)
            for r in range(SAMPLES // LANES)
        ]
        return jnp.concatenate([jnp.where(index == row, one, zero) for row in spread], axis=1)

    count_ref[...] = lax.dot_general(
        hot(place), hot(owner), NT, preferred_element_type=jnp.float32
    )


def chips_transform(parts_ref, group, twice):
    pair = jnp.concatenate(split(parts_ref[pl.ds(group, CHIPS, stride=8), :]), axis=0)
    return jnp.dot(twice, pair, preferred_element_type=jnp.float32)


def own_kernel(parts_ref, out_ref, turned_ref):
    scale = 1.0 / jnp.sqrt(jnp.float32(ROWS))
    twice = hadamard_twice()
    for group in range(8):
        done = chips_transform(parts_ref, group, twice)
        rows = slice(group * CHIPS, (group + 1) * CHIPS)
        done = done * scale
        out_ref[rows, :] = done
        turned_ref[rows, :] = done.T


def both_kernel(parts_ref, own_ref, turned_ref, count_ref, out_ref):
    scale = 1.0 / jnp.sqrt(jnp.float32(ROWS))
    side = (1 - 2 * lax.axis_index("core")).astype(jnp.float32)
    twice = hadamard_twice()
    sums, gaps = [], []
    for group in range(8):
        done = chips_transform(parts_ref, group, twice) * scale
        rows = slice(group * CHIPS, (group + 1) * CHIPS)
        out_ref[pl.ds(group, CHIPS, stride=WIDTH), :] = done + own_ref[rows, :] * side
        other, own = done.T, turned_ref[rows, :]
        sums.append(own + other)
        gaps.append(own - other)
    columns = []
    for turned in (sums, gaps):
        for b in range(BLOCKS):
            rows = slice(8 * (b % 16), 8 * (b % 16) + 8)
            columns.append(
                jnp.concatenate([turned[b // 16][rows, :], turned[4 + b // 16][rows, :]], axis=0)
            )
    counts = count_ref[...]
    weighed = [column * counts[b : b + 1, :] for b, column in enumerate(columns)]
    chunk = 2 * BLOCKS // CHUNKS

    def stacked(values):
        rows = []
        for c in range(CHUNKS):
            rows += split(jnp.concatenate(values[c * chunk : (c + 1) * chunk], axis=1))
        return jnp.concatenate(rows, axis=0)

    square = lax.dot_general(
        stacked(weighed), stacked(columns), NT, preferred_element_type=jnp.float32
    )
    lane_chunk = lax.broadcasted_iota(jnp.int32, (32, 32 * CHUNKS), 1) >> 5
    gram = jnp.zeros((32, 32 * CHUNKS), jnp.float32)
    for c in range(CHUNKS):
        gram = jnp.where(lane_chunk == c, square[32 * c : 32 * c + 32, :], gram)
    gram = gram[:COLUMNS, :] + gram[COLUMNS:, :]
    tiled = exact_pick(gram, columns_alike(32 * CHUNKS, LANES))
    lanes = lax.broadcasted_iota(jnp.int32, (COLUMNS, LANES), 1)
    rows = lax.broadcasted_iota(jnp.int32, (COLUMNS, LANES), 0)
    kept = jnp.where((lanes >> 4) == (rows & 7), tiled, 0.0)
    for half in range(2):
        flat = jnp.sum(kept[8 * half : 8 * half + 8, :], axis=0, keepdims=True)
        out_ref[pl.ds(8 + half, CHIPS, stride=WIDTH), :] = jnp.broadcast_to(flat, (CHIPS, LANES))


def place_kernel(parts_ref, out_hbm, gram_hbm, out_ref, gram_ref, sems):
    copies = []
    for half in range(2):
        for quarter in range(4):
            turned = parts_ref[pl.ds(4 * half + quarter, LANES, stride=WIDTH), :].T
            for b in range(16):
                block = quarter * 16 + b
                out_ref[half, :, block * LANES : (block + 1) * LANES] = turned[
                    8 * b : 8 * b + 8, :
                ]
        copies.append(
            pltpu.make_async_copy(
                out_ref.at[half], out_hbm.at[pl.ds(8 * half, 8), :], sems.at[half]
            )
        )
        copies[half].start()
    flat = [
        jnp.sum(parts_ref[pl.ds(8 + half, CHIPS, stride=WIDTH), :], axis=0, keepdims=True)
        for half in range(2)
    ]
    lanes = lax.broadcasted_iota(jnp.int32, (COLUMNS, LANES), 1)
    rows = lax.broadcasted_iota(jnp.int32, (COLUMNS, LANES), 0)
    spread = jnp.where(rows < 8, flat[0], flat[1])
    spread = jnp.where((lanes >> 4) == (rows & 7), spread, 0.0)
    gram_ref[...] = exact_pick(spread, columns_alike(LANES, COLUMNS)) / jnp.float32(SAMPLES)
    copies.append(pltpu.make_async_copy(gram_ref, gram_hbm, sems.at[2]))
    copies[2].start()
    for copy in copies:
        copy.wait()


def call(kernel, outs, operands, name, specs=None, out_specs=None, scratch=(), flops=0, limit=LIMIT):
    return pl.pallas_call(
        kernel,
        out_shape=outs,
        in_specs=specs or [VMEM] * len(operands),
        out_specs=out_specs or jax.tree.map(lambda _: VMEM, outs),
        scratch_shapes=scratch,
        compiler_params=pltpu.CompilerParams(vmem_limit_bytes=limit),
        cost_estimate=pl.CostEstimate(flops=flops, bytes_accessed=1 << 20, transcendentals=0),
        name=name,
    )(*operands)


def per_device(panel, signs, samples):
    f32 = jnp.float32
    whole = jax.ShapeDtypeStruct((1024, LANES), f32)
    exchange = lambda value: lax.all_to_all(value, CHIP_AXES, 0, 0, tiled=True)
    in_hbm = lambda value: pltpu.with_memory_space_constraint(value, pltpu.HBM)
    parts, samples = call(
        local_kernel,
        (pltpu.VMEM((1024, LANES), f32), pltpu.VMEM((LANES, LANES), jnp.int32)),
        (
            in_hbm(panel),
            in_hbm(signs.reshape(BLOCKS, LANES)),
            in_hbm(samples.reshape(LANES, LANES)),
        ),
        "local_transform",
        specs=[HBM] * 3,
        scratch=[
            pltpu.VMEM((2, 8, LOCAL_ROWS), f32),
            pltpu.VMEM((BLOCKS, LANES), jnp.int32),
            pltpu.SemaphoreType.DMA((4,)),
        ],
    )
    parts = exchange(parts.reshape(CHIPS, 8, LANES)).reshape(1024, LANES)
    parts, samples = lax.optimization_barrier((parts, samples))
    other = lax.ppermute(parts, "core", [(0, 1), (1, 0)])
    own, turned = call(own_kernel, (whole, whole), (parts,), "own_chips_transform", flops=1 << 28)
    counts = call(
        count_kernel,
        jax.ShapeDtypeStruct((2 * BLOCKS, CHIPS), f32),
        (samples,),
        "count_samples",
        flops=1 << 30,
    )
    back = call(
        both_kernel,
        jax.ShapeDtypeStruct((CHIPS * WIDTH, LANES), f32),
        (other, own, turned, counts),
        "both_cores",
    )
    back = exchange(back.reshape(CHIPS, 1, WIDTH * LANES)).reshape(CHIPS * WIDTH, LANES)
    return call(
        place_kernel,
        (
            jax.ShapeDtypeStruct((COLUMNS, LOCAL_ROWS), f32),
            jax.ShapeDtypeStruct((COLUMNS, COLUMNS), f32),
        ),
        (back,),
        "place_rows",
        out_specs=(HBM, HBM),
        scratch=[
            pltpu.VMEM((2, 8, LOCAL_ROWS), f32),
            pltpu.VMEM((COLUMNS, COLUMNS), f32),
            pltpu.SemaphoreType.DMA((3,)),
        ],
    )


def solution(mesh):
    wide, narrow = mesh.devices.shape
    split_mesh = Mesh(mesh.devices.reshape(wide, narrow // 2, 2), ALL_AXES)
    return jax.shard_map(
        per_device,
        mesh=split_mesh,
        in_specs=(P(None, ALL_AXES), P(ALL_AXES), P()),
        out_specs=(P(None, ALL_AXES), P()),
        check_vma=False,
    )
```

```python
import jax
import jax.numpy as jnp
from jax import lax
from jax.experimental import pallas as pl
from jax.experimental.pallas import tpu as pltpu
from jax.sharding import Mesh
from jax.sharding import PartitionSpec as P

COLUMNS = 16
LANES = 128
BLOCKS = 64
CHIPS = 128
LOCAL_ROWS = BLOCKS * LANES
ROWS = 2 * CHIPS * LOCAL_ROWS
SAMPLES = 16384
CHUNKS = 8
WIDTH = 10
CHIP_AXES = ("wide", "slow")
ALL_AXES = ("wide", "slow", "core")
NT = (((1,), (1,)), ((), ()))
VMEM = pl.BlockSpec(memory_space=pltpu.VMEM)
HBM = pl.BlockSpec(memory_space=pltpu.HBM)
LIMIT = 32 * 1024 * 1024


def hadamard_twice():
    first = lax.broadcasted_iota(jnp.int32, (LANES, LANES), 0)
    second = lax.broadcasted_iota(jnp.int32, (LANES, LANES), 1)
    bits = first & second
    bits = bits ^ (bits >> 4)
    bits = bits ^ (bits >> 2)
    bits = bits ^ (bits >> 1)
    had = jnp.where((bits & 1) == 0, 1.0, -1.0).astype(jnp.bfloat16)
    return jnp.concatenate([had, had], axis=1)


def split(value):
    high = value.astype(jnp.bfloat16)
    low = (value - high.astype(jnp.float32)).astype(jnp.bfloat16)
    return high, low


def columns_alike(rows, lanes):
    first = lax.broadcasted_iota(jnp.int32, (rows, lanes), 0)
    second = lax.broadcasted_iota(jnp.int32, (rows, lanes), 1)
    return jnp.where(((first ^ second) & 15) == 0, 1.0, 0.0).astype(jnp.bfloat16)


def exact_pick(value, ones):
    count = value.shape[0]
    high, low = split(value)
    rest = value - high.astype(jnp.float32) - low.astype(jnp.float32)
    parts = jnp.concatenate([high, low, rest.astype(jnp.bfloat16)], axis=0)
    done = jnp.dot(parts, ones, preferred_element_type=jnp.float32)
    return done[:count, :] + done[count : 2 * count, :] + done[2 * count :, :]


def butterfly(parts):
    step = 1
    while step < len(parts):
        parts = [
            parts[i] + parts[i + step] if i & step == 0 else parts[i - step] - parts[i]
            for i in range(len(parts))
        ]
        step *= 2
    return parts


def local_kernel(
    panel_hbm, signs_hbm, samples_hbm, out_ref, samples_ref, panel_ref, signs_ref, sems
):
    copies = [
        pltpu.make_async_copy(signs_hbm, signs_ref, sems.at[0]),
        pltpu.make_async_copy(panel_hbm, panel_ref, sems.at[1]),
        pltpu.make_async_copy(samples_hbm, samples_ref, sems.at[2]),
    ]
    for copy in copies:
        copy.start()
    twice = hadamard_twice()
    copies[0].wait()
    copies[1].wait()
    for half in range(2):
        signs = signs_ref[...].astype(jnp.float32)
        parts = [
            panel_ref[8 * half : 8 * half + 8, b * LANES : (b + 1) * LANES] * signs[b : b + 1, :]
            for b in range(BLOCKS)
        ]
        parts = butterfly(parts)
        for quarter in range(4):
            block = jnp.concatenate(parts[16 * quarter : 16 * quarter + 16], axis=0)
            pair = jnp.concatenate(split(block), axis=1)
            done = lax.dot_general(twice, pair, NT, preferred_element_type=jnp.float32)
            out_ref[pl.ds(4 * half + quarter, LANES, stride=8), :] = done
    copies[2].wait()


def count_kernel(samples_ref, count_ref):
    chip = lax.axis_index("wide") * lax.axis_size("slow") + lax.axis_index("slow")
    rows = samples_ref[...]
    place = ((rows >> 13) & 1) * BLOCKS + ((rows >> 7) & 63)
    place = jnp.where((rows & 127) == chip, place, -1).astype(jnp.float32)
    owner = (rows >> 14).astype(jnp.float32)
    index = lax.broadcasted_iota(jnp.int32, (CHIPS, LANES), 0)
    index = index.astype(jnp.float32).astype(jnp.bfloat16)
    one, zero = jnp.ones_like(index), jnp.zeros_like(index)

    def hot(values):
        spread = [
            jnp.broadcast_to(values[r : r + 1, :], index.shape).astype(jnp.bfloat16)
            for r in range(SAMPLES // LANES)
        ]
        return jnp.concatenate([jnp.where(index == row, one, zero) for row in spread], axis=1)

    count_ref[...] = lax.dot_general(
        hot(place), hot(owner), NT, preferred_element_type=jnp.float32
    )


def chips_transform(parts_ref, group, twice):
    pair = jnp.concatenate(split(parts_ref[pl.ds(group, CHIPS, stride=8), :]), axis=0)
    return jnp.dot(twice, pair, preferred_element_type=jnp.float32)


def own_kernel(parts_ref, out_ref, turned_ref):
    scale = 1.0 / jnp.sqrt(jnp.float32(ROWS))
    twice = hadamard_twice()
    for group in range(8):
        done = chips_transform(parts_ref, group, twice)
        rows = slice(group * CHIPS, (group + 1) * CHIPS)
        done = done * scale
        out_ref[rows, :] = done
        turned_ref[rows, :] = done.T


def both_kernel(parts_ref, own_ref, turned_ref, count_ref, out_ref):
    scale = 1.0 / jnp.sqrt(jnp.float32(ROWS))
    side = (1 - 2 * lax.axis_index("core")).astype(jnp.float32)
    twice = hadamard_twice()
    sums, gaps = [], []
    for group in range(8):
        done = chips_transform(parts_ref, group, twice) * scale
        rows = slice(group * CHIPS, (group + 1) * CHIPS)
        out_ref[pl.ds(group, CHIPS, stride=WIDTH), :] = done + own_ref[rows, :] * side
        other, own = done.T, turned_ref[rows, :]
        sums.append(own + other)
        gaps.append(own - other)
    columns = []
    for turned in (sums, gaps):
        for b in range(BLOCKS):
            rows = slice(8 * (b % 16), 8 * (b % 16) + 8)
            columns.append(
                jnp.concatenate([turned[b // 16][rows, :], turned[4 + b // 16][rows, :]], axis=0)
            )
    counts = count_ref[...]
    weighed = [column * counts[b : b + 1, :] for b, column in enumerate(columns)]
    chunk = 2 * BLOCKS // CHUNKS

    def stacked(values):
        rows = []
        for c in range(CHUNKS):
            rows += split(jnp.concatenate(values[c * chunk : (c + 1) * chunk], axis=1))
        return jnp.concatenate(rows, axis=0)

    square = lax.dot_general(
        stacked(weighed), stacked(columns), NT, preferred_element_type=jnp.float32
    )
    lane_chunk = lax.broadcasted_iota(jnp.int32, (32, 32 * CHUNKS), 1) >> 5
    gram = jnp.zeros((32, 32 * CHUNKS), jnp.float32)
    for c in range(CHUNKS):
        gram = jnp.where(lane_chunk == c, square[32 * c : 32 * c + 32, :], gram)
    gram = gram[:COLUMNS, :] + gram[COLUMNS:, :]
    tiled = exact_pick(gram, columns_alike(32 * CHUNKS, LANES))
    lanes = lax.broadcasted_iota(jnp.int32, (COLUMNS, LANES), 1)
    rows = lax.broadcasted_iota(jnp.int32, (COLUMNS, LANES), 0)
    kept = jnp.where((lanes >> 4) == (rows & 7), tiled, 0.0)
    for half in range(2):
        flat = jnp.sum(kept[8 * half : 8 * half + 8, :], axis=0, keepdims=True)
        out_ref[pl.ds(8 + half, CHIPS, stride=WIDTH), :] = jnp.broadcast_to(flat, (CHIPS, LANES))


def place_kernel(parts_ref, out_hbm, gram_hbm, out_ref, gram_ref, sems):
    copies = []
    for half in range(2):
        for quarter in range(4):
            turned = parts_ref[pl.ds(4 * half + quarter, LANES, stride=WIDTH), :].T
            for b in range(16):
                block = quarter * 16 + b
                out_ref[half, :, block * LANES : (block + 1) * LANES] = turned[
                    8 * b : 8 * b + 8, :
                ]
            if quarter % 2 == 1:
                lanes = pl.ds((quarter - 1) * 16 * LANES, 32 * LANES)
                copies.append(
                    pltpu.make_async_copy(
                        out_ref.at[half, :, lanes],
                        out_hbm.at[pl.ds(8 * half, 8), lanes],
                        sems.at[len(copies)],
                    )
                )
                copies[-1].start()
    flat = [
        jnp.sum(parts_ref[pl.ds(8 + half, CHIPS, stride=WIDTH), :], axis=0, keepdims=True)
        for half in range(2)
    ]
    lanes = lax.broadcasted_iota(jnp.int32, (COLUMNS, LANES), 1)
    rows = lax.broadcasted_iota(jnp.int32, (COLUMNS, LANES), 0)
    spread = jnp.where(rows < 8, flat[0], flat[1])
    spread = jnp.where((lanes >> 4) == (rows & 7), spread, 0.0)
    gram_ref[...] = exact_pick(spread, columns_alike(LANES, COLUMNS)) / jnp.float32(SAMPLES)
    copies.append(pltpu.make_async_copy(gram_ref, gram_hbm, sems.at[4]))
    copies[-1].start()
    for copy in copies:
        copy.wait()


def call(kernel, outs, operands, name, specs=None, out_specs=None, scratch=(), flops=0, limit=LIMIT):
    return pl.pallas_call(
        kernel,
        out_shape=outs,
        in_specs=specs or [VMEM] * len(operands),
        out_specs=out_specs or jax.tree.map(lambda _: VMEM, outs),
        scratch_shapes=scratch,
        compiler_params=pltpu.CompilerParams(vmem_limit_bytes=limit),
        cost_estimate=pl.CostEstimate(flops=flops, bytes_accessed=1 << 20, transcendentals=0),
        name=name,
    )(*operands)


def per_device(panel, signs, samples):
    f32 = jnp.float32
    whole = jax.ShapeDtypeStruct((1024, LANES), f32)
    exchange = lambda value: lax.all_to_all(value, CHIP_AXES, 0, 0, tiled=True)
    in_hbm = lambda value: pltpu.with_memory_space_constraint(value, pltpu.HBM)
    parts, samples = call(
        local_kernel,
        (pltpu.VMEM((1024, LANES), f32), pltpu.VMEM((LANES, LANES), jnp.int32)),
        (
            in_hbm(panel),
            in_hbm(signs.reshape(BLOCKS, LANES)),
            in_hbm(samples.reshape(LANES, LANES)),
        ),
        "local_transform",
        specs=[HBM] * 3,
        scratch=[
            pltpu.VMEM((COLUMNS, LOCAL_ROWS), f32),
            pltpu.VMEM((BLOCKS, LANES), jnp.int32),
            pltpu.SemaphoreType.DMA((3,)),
        ],
    )
    parts = exchange(parts.reshape(CHIPS, 8, LANES)).reshape(1024, LANES)
    parts, samples = lax.optimization_barrier((parts, samples))
    other = lax.ppermute(parts, "core", [(0, 1), (1, 0)])
    own, turned = call(own_kernel, (whole, whole), (parts,), "own_chips_transform", flops=1 << 28)
    counts = call(
        count_kernel,
        jax.ShapeDtypeStruct((2 * BLOCKS, CHIPS), f32),
        (samples,),
        "count_samples",
        flops=1 << 30,
    )
    back = call(
        both_kernel,
        jax.ShapeDtypeStruct((CHIPS * WIDTH, LANES), f32),
        (other, own, turned, counts),
        "both_cores",
    )
    back = exchange(back.reshape(CHIPS, 1, WIDTH * LANES)).reshape(CHIPS * WIDTH, LANES)
    return call(
        place_kernel,
        (
            jax.ShapeDtypeStruct((COLUMNS, LOCAL_ROWS), f32),
            jax.ShapeDtypeStruct((COLUMNS, COLUMNS), f32),
        ),
        (back,),
        "place_rows",
        out_specs=(HBM, HBM),
        scratch=[
            pltpu.VMEM((2, 8, LOCAL_ROWS), f32),
            pltpu.VMEM((COLUMNS, COLUMNS), f32),
            pltpu.SemaphoreType.DMA((5,)),
        ],
    )


def solution(mesh):
    wide, narrow = mesh.devices.shape
    split_mesh = Mesh(mesh.devices.reshape(wide, narrow // 2, 2), ALL_AXES)
    return jax.shard_map(
        per_device,
        mesh=split_mesh,
        in_specs=(P(None, ALL_AXES), P(ALL_AXES), P()),
        out_specs=(P(None, ALL_AXES), P()),
        check_vma=False,
    )
```

```python
import jax
import jax.numpy as jnp
from jax import lax
from jax.experimental import pallas as pl
from jax.experimental.pallas import tpu as pltpu
from jax.sharding import Mesh
from jax.sharding import PartitionSpec as P

COLUMNS = 16
LANES = 128
BLOCKS = 64
CHIPS = 128
LOCAL_ROWS = BLOCKS * LANES
ROWS = 2 * CHIPS * LOCAL_ROWS
SAMPLES = 16384
CHUNKS = 8
WIDTH = 10
OUT_AXES = ("wide", "slow")
BACK_AXES = ("slow", "wide")
ALL_AXES = ("wide", "slow", "core")
NT = (((1,), (1,)), ((), ()))
VMEM = pl.BlockSpec(memory_space=pltpu.VMEM)
HBM = pl.BlockSpec(memory_space=pltpu.HBM)
LIMIT = 32 * 1024 * 1024


def there(chip):
    return ((chip & 7) << 4) | (chip >> 3)


def back_again(chip):
    return ((chip & 15) << 3) | (chip >> 4)


def hadamard_twice(row_of):
    first = row_of(lax.broadcasted_iota(jnp.int32, (LANES, LANES), 0))
    second = lax.broadcasted_iota(jnp.int32, (LANES, LANES), 1)
    bits = first & second
    bits = bits ^ (bits >> 4)
    bits = bits ^ (bits >> 2)
    bits = bits ^ (bits >> 1)
    had = jnp.where((bits & 1) == 0, 1.0, -1.0).astype(jnp.bfloat16)
    return jnp.concatenate([had, had], axis=1)


def split(value):
    high = value.astype(jnp.bfloat16)
    low = (value - high.astype(jnp.float32)).astype(jnp.bfloat16)
    return high, low


def columns_alike(rows, lanes):
    first = lax.broadcasted_iota(jnp.int32, (rows, lanes), 0)
    second = lax.broadcasted_iota(jnp.int32, (rows, lanes), 1)
    return jnp.where(((first ^ second) & 15) == 0, 1.0, 0.0).astype(jnp.bfloat16)


def exact_pick(value, ones):
    count = value.shape[0]
    high, low = split(value)
    rest = value - high.astype(jnp.float32) - low.astype(jnp.float32)
    parts = jnp.concatenate([high, low, rest.astype(jnp.bfloat16)], axis=0)
    done = jnp.dot(parts, ones, preferred_element_type=jnp.float32)
    return done[:count, :] + done[count : 2 * count, :] + done[2 * count :, :]


def butterfly(parts):
    step = 1
    while step < len(parts):
        parts = [
            parts[i] + parts[i + step] if i & step == 0 else parts[i - step] - parts[i]
            for i in range(len(parts))
        ]
        step *= 2
    return parts


def local_kernel(
    panel_hbm, signs_hbm, samples_hbm, out_ref, samples_ref, panel_ref, signs_ref, sems
):
    copies = [
        pltpu.make_async_copy(signs_hbm, signs_ref, sems.at[0]),
        pltpu.make_async_copy(panel_hbm, panel_ref, sems.at[1]),
        pltpu.make_async_copy(samples_hbm, samples_ref, sems.at[2]),
    ]
    for copy in copies:
        copy.start()
    twice = hadamard_twice(there)
    copies[0].wait()
    copies[1].wait()
    for half in range(2):
        signs = signs_ref[...].astype(jnp.float32)
        parts = [
            panel_ref[8 * half : 8 * half + 8, b * LANES : (b + 1) * LANES] * signs[b : b + 1, :]
            for b in range(BLOCKS)
        ]
        parts = butterfly(parts)
        for quarter in range(4):
            block = jnp.concatenate(parts[16 * quarter : 16 * quarter + 16], axis=0)
            pair = jnp.concatenate(split(block), axis=1)
            done = lax.dot_general(twice, pair, NT, preferred_element_type=jnp.float32)
            out_ref[pl.ds(4 * half + quarter, LANES, stride=8), :] = done
    copies[2].wait()


def count_kernel(samples_ref, count_ref):
    chip = lax.axis_index("slow") * lax.axis_size("wide") + lax.axis_index("wide")
    rows = samples_ref[...]
    place = ((rows >> 13) & 1) * BLOCKS + ((rows >> 7) & 63)
    place = jnp.where((rows & 127) == chip, place, -1).astype(jnp.float32)
    owner = there(rows >> 14).astype(jnp.float32)
    index = lax.broadcasted_iota(jnp.int32, (CHIPS, LANES), 0)
    index = index.astype(jnp.float32).astype(jnp.bfloat16)
    one, zero = jnp.ones_like(index), jnp.zeros_like(index)

    def hot(values):
        spread = [
            jnp.broadcast_to(values[r : r + 1, :], index.shape).astype(jnp.bfloat16)
            for r in range(SAMPLES // LANES)
        ]
        return jnp.concatenate([jnp.where(index == row, one, zero) for row in spread], axis=1)

    count_ref[...] = lax.dot_general(
        hot(place), hot(owner), NT, preferred_element_type=jnp.float32
    )


def chips_transform(parts_ref, group, twice):
    pair = jnp.concatenate(split(parts_ref[pl.ds(group, CHIPS, stride=8), :]), axis=0)
    return jnp.dot(twice, pair, preferred_element_type=jnp.float32)


def own_kernel(parts_ref, out_ref, turned_ref):
    scale = 1.0 / jnp.sqrt(jnp.float32(ROWS))
    twice = hadamard_twice(back_again)
    for group in range(8):
        done = chips_transform(parts_ref, group, twice)
        rows = slice(group * CHIPS, (group + 1) * CHIPS)
        done = done * scale
        out_ref[rows, :] = done
        turned_ref[rows, :] = done.T


def both_kernel(parts_ref, own_ref, turned_ref, count_ref, out_ref):
    scale = 1.0 / jnp.sqrt(jnp.float32(ROWS))
    side = (1 - 2 * lax.axis_index("core")).astype(jnp.float32)
    twice = hadamard_twice(back_again)
    sums, gaps = [], []
    for group in range(8):
        done = chips_transform(parts_ref, group, twice) * scale
        rows = slice(group * CHIPS, (group + 1) * CHIPS)
        out_ref[pl.ds(group, CHIPS, stride=WIDTH), :] = done + own_ref[rows, :] * side
        other, own = done.T, turned_ref[rows, :]
        sums.append(own + other)
        gaps.append(own - other)
    columns = []
    for turned in (sums, gaps):
        for b in range(BLOCKS):
            rows = slice(8 * (b % 16), 8 * (b % 16) + 8)
            columns.append(
                jnp.concatenate([turned[b // 16][rows, :], turned[4 + b // 16][rows, :]], axis=0)
            )
    counts = count_ref[...]
    weighed = [column * counts[b : b + 1, :] for b, column in enumerate(columns)]
    chunk = 2 * BLOCKS // CHUNKS

    def stacked(values):
        rows = []
        for c in range(CHUNKS):
            rows += split(jnp.concatenate(values[c * chunk : (c + 1) * chunk], axis=1))
        return jnp.concatenate(rows, axis=0)

    square = lax.dot_general(
        stacked(weighed), stacked(columns), NT, preferred_element_type=jnp.float32
    )
    lane_chunk = lax.broadcasted_iota(jnp.int32, (32, 32 * CHUNKS), 1) >> 5
    gram = jnp.zeros((32, 32 * CHUNKS), jnp.float32)
    for c in range(CHUNKS):
        gram = jnp.where(lane_chunk == c, square[32 * c : 32 * c + 32, :], gram)
    gram = gram[:COLUMNS, :] + gram[COLUMNS:, :]
    tiled = exact_pick(gram, columns_alike(32 * CHUNKS, LANES))
    lanes = lax.broadcasted_iota(jnp.int32, (COLUMNS, LANES), 1)
    rows = lax.broadcasted_iota(jnp.int32, (COLUMNS, LANES), 0)
    kept = jnp.where((lanes >> 4) == (rows & 7), tiled, 0.0)
    for half in range(2):
        flat = jnp.sum(kept[8 * half : 8 * half + 8, :], axis=0, keepdims=True)
        out_ref[pl.ds(8 + half, CHIPS, stride=WIDTH), :] = jnp.broadcast_to(flat, (CHIPS, LANES))


def place_kernel(parts_ref, out_hbm, gram_hbm, out_ref, gram_ref, sems):
    copies = []
    for half in range(2):
        for quarter in range(4):
            turned = parts_ref[pl.ds(4 * half + quarter, LANES, stride=WIDTH), :].T
            for b in range(16):
                block = quarter * 16 + b
                out_ref[half, :, block * LANES : (block + 1) * LANES] = turned[
                    8 * b : 8 * b + 8, :
                ]
            if quarter % 2 == 1:
                lanes = pl.ds((quarter - 1) * 16 * LANES, 32 * LANES)
                copies.append(
                    pltpu.make_async_copy(
                        out_ref.at[half, :, lanes],
                        out_hbm.at[pl.ds(8 * half, 8), lanes],
                        sems.at[len(copies)],
                    )
                )
                copies[-1].start()
    flat = [
        jnp.sum(parts_ref[pl.ds(8 + half, CHIPS, stride=WIDTH), :], axis=0, keepdims=True)
        for half in range(2)
    ]
    lanes = lax.broadcasted_iota(jnp.int32, (COLUMNS, LANES), 1)
    rows = lax.broadcasted_iota(jnp.int32, (COLUMNS, LANES), 0)
    spread = jnp.where(rows < 8, flat[0], flat[1])
    spread = jnp.where((lanes >> 4) == (rows & 7), spread, 0.0)
    gram_ref[...] = exact_pick(spread, columns_alike(LANES, COLUMNS)) / jnp.float32(SAMPLES)
    copies.append(pltpu.make_async_copy(gram_ref, gram_hbm, sems.at[4]))
    copies[-1].start()
    for copy in copies:
        copy.wait()


def call(kernel, outs, operands, name, specs=None, out_specs=None, scratch=(), flops=0, limit=LIMIT):
    return pl.pallas_call(
        kernel,
        out_shape=outs,
        in_specs=specs or [VMEM] * len(operands),
        out_specs=out_specs or jax.tree.map(lambda _: VMEM, outs),
        scratch_shapes=scratch,
        compiler_params=pltpu.CompilerParams(vmem_limit_bytes=limit),
        cost_estimate=pl.CostEstimate(flops=flops, bytes_accessed=1 << 20, transcendentals=0),
        name=name,
    )(*operands)


def per_device(panel, signs, samples):
    f32 = jnp.float32
    whole = jax.ShapeDtypeStruct((1024, LANES), f32)
    exchange = lambda value, axes: lax.all_to_all(value, axes, 0, 0, tiled=True)
    in_hbm = lambda value: pltpu.with_memory_space_constraint(value, pltpu.HBM)
    parts, samples = call(
        local_kernel,
        (pltpu.VMEM((1024, LANES), f32), pltpu.VMEM((LANES, LANES), jnp.int32)),
        (
            in_hbm(panel),
            in_hbm(signs.reshape(BLOCKS, LANES)),
            in_hbm(samples.reshape(LANES, LANES)),
        ),
        "local_transform",
        specs=[HBM] * 3,
        scratch=[
            pltpu.VMEM((COLUMNS, LOCAL_ROWS), f32),
            pltpu.VMEM((BLOCKS, LANES), jnp.int32),
            pltpu.SemaphoreType.DMA((3,)),
        ],
    )
    parts = exchange(parts.reshape(CHIPS, 8, LANES), OUT_AXES).reshape(1024, LANES)
    parts, samples = lax.optimization_barrier((parts, samples))
    other = lax.ppermute(parts, "core", [(0, 1), (1, 0)])
    own, turned = call(own_kernel, (whole, whole), (parts,), "own_chips_transform", flops=1 << 28)
    counts = call(
        count_kernel,
        jax.ShapeDtypeStruct((2 * BLOCKS, CHIPS), f32),
        (samples,),
        "count_samples",
        flops=1 << 30,
    )
    back = call(
        both_kernel,
        jax.ShapeDtypeStruct((CHIPS * WIDTH, LANES), f32),
        (other, own, turned, counts),
        "both_cores",
    )
    back = exchange(back.reshape(CHIPS, 1, WIDTH * LANES), BACK_AXES)
    back = back.reshape(CHIPS * WIDTH, LANES)
    return call(
        place_kernel,
        (
            jax.ShapeDtypeStruct((COLUMNS, LOCAL_ROWS), f32),
            jax.ShapeDtypeStruct((COLUMNS, COLUMNS), f32),
        ),
        (back,),
        "place_rows",
        out_specs=(HBM, HBM),
        scratch=[
            pltpu.VMEM((2, 8, LOCAL_ROWS), f32),
            pltpu.VMEM((COLUMNS, COLUMNS), f32),
            pltpu.SemaphoreType.DMA((5,)),
        ],
    )


def solution(mesh):
    wide, narrow = mesh.devices.shape
    split_mesh = Mesh(mesh.devices.reshape(wide, narrow // 2, 2), ALL_AXES)
    return jax.shard_map(
        per_device,
        mesh=split_mesh,
        in_specs=(P(None, ALL_AXES), P(ALL_AXES), P()),
        out_specs=(P(None, ALL_AXES), P()),
        check_vma=False,
    )
```

```python
import jax
import jax.numpy as jnp
from jax import lax
from jax.experimental import pallas as pl
from jax.experimental.pallas import tpu as pltpu
from jax.sharding import Mesh
from jax.sharding import PartitionSpec as P

COLUMNS = 16
LANES = 128
BLOCKS = 64
CHIPS = 128
LOCAL_ROWS = BLOCKS * LANES
ROWS = 2 * CHIPS * LOCAL_ROWS
SAMPLES = 16384
CHUNKS = 8
WIDTH = 10
OUT_AXES = ("wide", "slow")
BACK_AXES = ("slow", "wide")
ALL_AXES = ("wide", "slow", "core")
NT = (((1,), (1,)), ((), ()))
VMEM = pl.BlockSpec(memory_space=pltpu.VMEM)
HBM = pl.BlockSpec(memory_space=pltpu.HBM)
LIMIT = 32 * 1024 * 1024


def there(chip):
    return ((chip & 7) << 4) | (chip >> 3)


def back_again(chip):
    return ((chip & 15) << 3) | (chip >> 4)


def hadamard_twice(row_of):
    first = row_of(lax.broadcasted_iota(jnp.int32, (LANES, LANES), 0))
    second = lax.broadcasted_iota(jnp.int32, (LANES, LANES), 1)
    bits = first & second
    bits = bits ^ (bits >> 4)
    bits = bits ^ (bits >> 2)
    bits = bits ^ (bits >> 1)
    had = jnp.where((bits & 1) == 0, 1.0, -1.0).astype(jnp.bfloat16)
    return jnp.concatenate([had, had], axis=1)


def split(value):
    high = value.astype(jnp.bfloat16)
    low = (value - high.astype(jnp.float32)).astype(jnp.bfloat16)
    return high, low


def columns_alike(rows, lanes):
    first = lax.broadcasted_iota(jnp.int32, (rows, lanes), 0)
    second = lax.broadcasted_iota(jnp.int32, (rows, lanes), 1)
    return jnp.where(((first ^ second) & 15) == 0, 1.0, 0.0).astype(jnp.bfloat16)


def exact_pick(value, ones):
    count = value.shape[0]
    high, low = split(value)
    rest = value - high.astype(jnp.float32) - low.astype(jnp.float32)
    parts = jnp.concatenate([high, low, rest.astype(jnp.bfloat16)], axis=0)
    done = jnp.dot(parts, ones, preferred_element_type=jnp.float32)
    return done[:count, :] + done[count : 2 * count, :] + done[2 * count :, :]


def butterfly(parts):
    step = 1
    while step < len(parts):
        parts = [
            parts[i] + parts[i + step] if i & step == 0 else parts[i - step] - parts[i]
            for i in range(len(parts))
        ]
        step *= 2
    return parts


def local_kernel(
    panel_hbm, signs_hbm, samples_hbm, out_ref, samples_ref, panel_ref, signs_ref, sems
):
    copies = [
        pltpu.make_async_copy(signs_hbm, signs_ref, sems.at[0]),
        pltpu.make_async_copy(panel_hbm, panel_ref, sems.at[1]),
        pltpu.make_async_copy(samples_hbm, samples_ref, sems.at[2]),
    ]
    for copy in copies:
        copy.start()
    twice = hadamard_twice(there)
    copies[0].wait()
    copies[1].wait()
    for half in range(2):
        signs = signs_ref[...].astype(jnp.float32)
        parts = [
            panel_ref[8 * half : 8 * half + 8, b * LANES : (b + 1) * LANES] * signs[b : b + 1, :]
            for b in range(BLOCKS)
        ]
        parts = butterfly(parts)
        for quarter in range(4):
            block = jnp.concatenate(parts[16 * quarter : 16 * quarter + 16], axis=0)
            pair = jnp.concatenate(split(block), axis=1)
            done = lax.dot_general(twice, pair, NT, preferred_element_type=jnp.float32)
            out_ref[pl.ds(4 * half + quarter, LANES, stride=8), :] = done
    copies[2].wait()


def count_kernel(samples_ref, count_ref):
    chip = lax.axis_index("slow") * lax.axis_size("wide") + lax.axis_index("wide")
    rows = samples_ref[...]
    place = ((rows >> 13) & 1) * BLOCKS + ((rows >> 7) & 63)
    place = jnp.where((rows & 127) == chip, place, -1).astype(jnp.float32)
    owner = there(rows >> 14).astype(jnp.float32)
    index = lax.broadcasted_iota(jnp.int32, (CHIPS, LANES), 0)
    index = index.astype(jnp.float32).astype(jnp.bfloat16)
    one, zero = jnp.ones_like(index), jnp.zeros_like(index)

    def hot(values):
        spread = [
            jnp.broadcast_to(values[r : r + 1, :], index.shape).astype(jnp.bfloat16)
            for r in range(SAMPLES // LANES)
        ]
        return jnp.concatenate([jnp.where(index == row, one, zero) for row in spread], axis=1)

    count_ref[...] = lax.dot_general(
        hot(place), hot(owner), NT, preferred_element_type=jnp.float32
    )


def chips_transform(parts_ref, group, twice):
    pair = jnp.concatenate(split(parts_ref[pl.ds(group, CHIPS, stride=8), :]), axis=0)
    return jnp.dot(twice, pair, preferred_element_type=jnp.float32)


def own_kernel(parts_ref, out_ref, turned_ref):
    scale = 1.0 / jnp.sqrt(jnp.float32(ROWS))
    twice = hadamard_twice(back_again)
    for group in range(8):
        done = chips_transform(parts_ref, group, twice)
        rows = slice(group * CHIPS, (group + 1) * CHIPS)
        done = done * scale
        out_ref[rows, :] = done
        turned_ref[rows, :] = done.T


def beside_kernel(parts_ref, samples_ref, out_ref, turned_ref, count_ref):
    own_kernel(parts_ref, out_ref, turned_ref)
    count_kernel(samples_ref, count_ref)


def both_kernel(parts_ref, own_ref, turned_ref, count_ref, out_ref):
    scale = 1.0 / jnp.sqrt(jnp.float32(ROWS))
    side = (1 - 2 * lax.axis_index("core")).astype(jnp.float32)
    twice = hadamard_twice(back_again)
    sums, gaps = [], []
    for group in range(8):
        done = chips_transform(parts_ref, group, twice) * scale
        rows = slice(group * CHIPS, (group + 1) * CHIPS)
        out_ref[pl.ds(group, CHIPS, stride=WIDTH), :] = done + own_ref[rows, :] * side
        other, own = done.T, turned_ref[rows, :]
        sums.append(own + other)
        gaps.append(own - other)
    columns = []
    for turned in (sums, gaps):
        for b in range(BLOCKS):
            rows = slice(8 * (b % 16), 8 * (b % 16) + 8)
            columns.append(
                jnp.concatenate([turned[b // 16][rows, :], turned[4 + b // 16][rows, :]], axis=0)
            )
    counts = count_ref[...]
    weighed = [column * counts[b : b + 1, :] for b, column in enumerate(columns)]
    chunk = 2 * BLOCKS // CHUNKS

    def stacked(values):
        rows = []
        for c in range(CHUNKS):
            rows += split(jnp.concatenate(values[c * chunk : (c + 1) * chunk], axis=1))
        return jnp.concatenate(rows, axis=0)

    square = lax.dot_general(
        stacked(weighed), stacked(columns), NT, preferred_element_type=jnp.float32
    )
    lane_chunk = lax.broadcasted_iota(jnp.int32, (32, 32 * CHUNKS), 1) >> 5
    gram = jnp.zeros((32, 32 * CHUNKS), jnp.float32)
    for c in range(CHUNKS):
        gram = jnp.where(lane_chunk == c, square[32 * c : 32 * c + 32, :], gram)
    gram = gram[:COLUMNS, :] + gram[COLUMNS:, :]
    tiled = exact_pick(gram, columns_alike(32 * CHUNKS, LANES))
    lanes = lax.broadcasted_iota(jnp.int32, (COLUMNS, LANES), 1)
    rows = lax.broadcasted_iota(jnp.int32, (COLUMNS, LANES), 0)
    kept = jnp.where((lanes >> 4) == (rows & 7), tiled, 0.0)
    for half in range(2):
        flat = jnp.sum(kept[8 * half : 8 * half + 8, :], axis=0, keepdims=True)
        out_ref[pl.ds(8 + half, CHIPS, stride=WIDTH), :] = jnp.broadcast_to(flat, (CHIPS, LANES))


def place_kernel(parts_ref, out_hbm, gram_hbm, out_ref, gram_ref, sems):
    copies = []
    for half in range(2):
        for quarter in range(4):
            turned = parts_ref[pl.ds(4 * half + quarter, LANES, stride=WIDTH), :].T
            for b in range(16):
                block = quarter * 16 + b
                out_ref[half, :, block * LANES : (block + 1) * LANES] = turned[
                    8 * b : 8 * b + 8, :
                ]
            if quarter % 2 == 1:
                lanes = pl.ds((quarter - 1) * 16 * LANES, 32 * LANES)
                copies.append(
                    pltpu.make_async_copy(
                        out_ref.at[half, :, lanes],
                        out_hbm.at[pl.ds(8 * half, 8), lanes],
                        sems.at[len(copies)],
                    )
                )
                copies[-1].start()
    flat = [
        jnp.sum(parts_ref[pl.ds(8 + half, CHIPS, stride=WIDTH), :], axis=0, keepdims=True)
        for half in range(2)
    ]
    lanes = lax.broadcasted_iota(jnp.int32, (COLUMNS, LANES), 1)
    rows = lax.broadcasted_iota(jnp.int32, (COLUMNS, LANES), 0)
    spread = jnp.where(rows < 8, flat[0], flat[1])
    spread = jnp.where((lanes >> 4) == (rows & 7), spread, 0.0)
    gram_ref[...] = exact_pick(spread, columns_alike(LANES, COLUMNS)) / jnp.float32(SAMPLES)
    copies.append(pltpu.make_async_copy(gram_ref, gram_hbm, sems.at[4]))
    copies[-1].start()
    for copy in copies:
        copy.wait()


def call(kernel, outs, operands, name, specs=None, out_specs=None, scratch=(), flops=0, limit=LIMIT):
    return pl.pallas_call(
        kernel,
        out_shape=outs,
        in_specs=specs or [VMEM] * len(operands),
        out_specs=out_specs or jax.tree.map(lambda _: VMEM, outs),
        scratch_shapes=scratch,
        compiler_params=pltpu.CompilerParams(vmem_limit_bytes=limit),
        cost_estimate=pl.CostEstimate(flops=flops, bytes_accessed=1 << 20, transcendentals=0),
        name=name,
    )(*operands)


def per_device(panel, signs, samples):
    f32 = jnp.float32
    whole = jax.ShapeDtypeStruct((1024, LANES), f32)
    exchange = lambda value, axes: lax.all_to_all(value, axes, 0, 0, tiled=True)
    in_hbm = lambda value: pltpu.with_memory_space_constraint(value, pltpu.HBM)
    parts, samples = call(
        local_kernel,
        (pltpu.VMEM((1024, LANES), f32), pltpu.VMEM((LANES, LANES), jnp.int32)),
        (
            in_hbm(panel),
            in_hbm(signs.reshape(BLOCKS, LANES)),
            in_hbm(samples.reshape(LANES, LANES)),
        ),
        "local_transform",
        specs=[HBM] * 3,
        scratch=[
            pltpu.VMEM((COLUMNS, LOCAL_ROWS), f32),
            pltpu.VMEM((BLOCKS, LANES), jnp.int32),
            pltpu.SemaphoreType.DMA((3,)),
        ],
    )
    parts = exchange(parts.reshape(CHIPS, 8, LANES), OUT_AXES).reshape(1024, LANES)
    parts, samples = lax.optimization_barrier((parts, samples))
    other = lax.ppermute(parts, "core", [(0, 1), (1, 0)])
    own, turned, counts = call(
        beside_kernel,
        (whole, whole, jax.ShapeDtypeStruct((2 * BLOCKS, CHIPS), f32)),
        (parts, samples),
        "own_and_counts",
        flops=1 << 30,
    )
    back = call(
        both_kernel,
        jax.ShapeDtypeStruct((CHIPS * WIDTH, LANES), f32),
        (other, own, turned, counts),
        "both_cores",
    )
    back = exchange(back.reshape(CHIPS, 1, WIDTH * LANES), BACK_AXES)
    back = back.reshape(CHIPS * WIDTH, LANES)
    return call(
        place_kernel,
        (
            jax.ShapeDtypeStruct((COLUMNS, LOCAL_ROWS), f32),
            jax.ShapeDtypeStruct((COLUMNS, COLUMNS), f32),
        ),
        (back,),
        "place_rows",
        out_specs=(HBM, HBM),
        scratch=[
            pltpu.VMEM((2, 8, LOCAL_ROWS), f32),
            pltpu.VMEM((COLUMNS, COLUMNS), f32),
            pltpu.SemaphoreType.DMA((5,)),
        ],
    )


def solution(mesh):
    wide, narrow = mesh.devices.shape
    split_mesh = Mesh(mesh.devices.reshape(wide, narrow // 2, 2), ALL_AXES)
    return jax.shard_map(
        per_device,
        mesh=split_mesh,
        in_specs=(P(None, ALL_AXES), P(ALL_AXES), P()),
        out_specs=(P(None, ALL_AXES), P()),
        check_vma=False,
    )
```

```python
import jax
import jax.numpy as jnp
from jax import lax
from jax.experimental import pallas as pl
from jax.experimental.pallas import tpu as pltpu
from jax.sharding import Mesh
from jax.sharding import PartitionSpec as P

COLUMNS = 16
LANES = 128
BLOCKS = 64
CHIPS = 128
LOCAL_ROWS = BLOCKS * LANES
ROWS = 2 * CHIPS * LOCAL_ROWS
SAMPLES = 16384
CHUNKS = 8
WIDTH = 10
OUT_AXES = ("wide", "slow")
BACK_AXES = ("slow", "wide")
ALL_AXES = ("wide", "slow", "core")
NT = (((1,), (1,)), ((), ()))
VMEM = pl.BlockSpec(memory_space=pltpu.VMEM)
HBM = pl.BlockSpec(memory_space=pltpu.HBM)
LIMIT = 32 * 1024 * 1024


def there(chip):
    return ((chip & 7) << 4) | (chip >> 3)


def back_again(chip):
    return ((chip & 15) << 3) | (chip >> 4)


def hadamard_twice(row_of):
    first = row_of(lax.broadcasted_iota(jnp.int32, (LANES, LANES), 0))
    second = lax.broadcasted_iota(jnp.int32, (LANES, LANES), 1)
    bits = first & second
    bits = bits ^ (bits >> 4)
    bits = bits ^ (bits >> 2)
    bits = bits ^ (bits >> 1)
    had = jnp.where((bits & 1) == 0, 1.0, -1.0).astype(jnp.bfloat16)
    return jnp.concatenate([had, had], axis=1)


def split(value):
    high = value.astype(jnp.bfloat16)
    low = (value - high.astype(jnp.float32)).astype(jnp.bfloat16)
    return high, low


def columns_alike(rows, lanes):
    first = lax.broadcasted_iota(jnp.int32, (rows, lanes), 0)
    second = lax.broadcasted_iota(jnp.int32, (rows, lanes), 1)
    return jnp.where(((first ^ second) & 15) == 0, 1.0, 0.0).astype(jnp.bfloat16)


def exact_pick(value, ones):
    count = value.shape[0]
    high, low = split(value)
    rest = value - high.astype(jnp.float32) - low.astype(jnp.float32)
    parts = jnp.concatenate([high, low, rest.astype(jnp.bfloat16)], axis=0)
    done = jnp.dot(parts, ones, preferred_element_type=jnp.float32)
    return done[:count, :] + done[count : 2 * count, :] + done[2 * count :, :]


def butterfly(parts):
    step = 1
    while step < len(parts):
        parts = [
            parts[i] + parts[i + step] if i & step == 0 else parts[i - step] - parts[i]
            for i in range(len(parts))
        ]
        step *= 2
    return parts


def local_kernel(
    panel_hbm, signs_hbm, samples_hbm, out_ref, samples_ref, panel_ref, signs_ref, sems
):
    copies = [
        pltpu.make_async_copy(signs_hbm, signs_ref, sems.at[0]),
        pltpu.make_async_copy(panel_hbm, panel_ref, sems.at[1]),
        pltpu.make_async_copy(samples_hbm, samples_ref, sems.at[2]),
    ]
    for index in (1, 0, 2):
        copies[index].start()
    twice = hadamard_twice(there)
    copies[0].wait()
    copies[1].wait()
    for half in range(2):
        signs = signs_ref[...].astype(jnp.float32)
        parts = [
            panel_ref[8 * half : 8 * half + 8, b * LANES : (b + 1) * LANES] * signs[b : b + 1, :]
            for b in range(BLOCKS)
        ]
        parts = butterfly(parts)
        for quarter in range(4):
            block = jnp.concatenate(parts[16 * quarter : 16 * quarter + 16], axis=0)
            pair = jnp.concatenate(split(block), axis=1)
            done = lax.dot_general(twice, pair, NT, preferred_element_type=jnp.float32)
            out_ref[pl.ds(4 * half + quarter, LANES, stride=8), :] = done
    copies[2].wait()


def count_kernel(samples_ref, count_ref):
    chip = lax.axis_index("slow") * lax.axis_size("wide") + lax.axis_index("wide")
    rows = samples_ref[...]
    place = ((rows >> 13) & 1) * BLOCKS + ((rows >> 7) & 63)
    place = jnp.where((rows & 127) == chip, place, -1).astype(jnp.float32)
    owner = there(rows >> 14).astype(jnp.float32)
    index = lax.broadcasted_iota(jnp.int32, (CHIPS, LANES), 0)
    index = index.astype(jnp.float32).astype(jnp.bfloat16)
    one, zero = jnp.ones_like(index), jnp.zeros_like(index)

    def hot(values):
        spread = [
            jnp.broadcast_to(values[r : r + 1, :], index.shape).astype(jnp.bfloat16)
            for r in range(SAMPLES // LANES)
        ]
        return jnp.concatenate([jnp.where(index == row, one, zero) for row in spread], axis=1)

    count_ref[...] = lax.dot_general(
        hot(place), hot(owner), NT, preferred_element_type=jnp.float32
    )


def chips_transform(parts_ref, group, twice):
    pair = jnp.concatenate(split(parts_ref[pl.ds(group, CHIPS, stride=8), :]), axis=0)
    return jnp.dot(twice, pair, preferred_element_type=jnp.float32)


def own_kernel(parts_ref, out_ref, turned_ref):
    scale = 1.0 / jnp.sqrt(jnp.float32(ROWS))
    twice = hadamard_twice(back_again)
    for group in range(8):
        done = chips_transform(parts_ref, group, twice)
        rows = slice(group * CHIPS, (group + 1) * CHIPS)
        done = done * scale
        out_ref[rows, :] = done
        turned_ref[rows, :] = done.T


def beside_kernel(parts_ref, samples_ref, out_ref, turned_ref, count_ref):
    own_kernel(parts_ref, out_ref, turned_ref)
    count_kernel(samples_ref, count_ref)


def both_kernel(parts_ref, own_ref, turned_ref, count_ref, out_ref):
    scale = 1.0 / jnp.sqrt(jnp.float32(ROWS))
    side = (1 - 2 * lax.axis_index("core")).astype(jnp.float32)
    twice = hadamard_twice(back_again)
    sums, gaps = [], []
    for group in range(8):
        done = chips_transform(parts_ref, group, twice) * scale
        rows = slice(group * CHIPS, (group + 1) * CHIPS)
        out_ref[pl.ds(group, CHIPS, stride=WIDTH), :] = done + own_ref[rows, :] * side
        other, own = done.T, turned_ref[rows, :]
        sums.append(own + other)
        gaps.append(own - other)
    columns = []
    for turned in (sums, gaps):
        for b in range(BLOCKS):
            rows = slice(8 * (b % 16), 8 * (b % 16) + 8)
            columns.append(
                jnp.concatenate([turned[b // 16][rows, :], turned[4 + b // 16][rows, :]], axis=0)
            )
    counts = count_ref[...]
    weighed = [column * counts[b : b + 1, :] for b, column in enumerate(columns)]
    chunk = 2 * BLOCKS // CHUNKS

    def stacked(values):
        rows = []
        for c in range(CHUNKS):
            rows += split(jnp.concatenate(values[c * chunk : (c + 1) * chunk], axis=1))
        return jnp.concatenate(rows, axis=0)

    square = lax.dot_general(
        stacked(weighed), stacked(columns), NT, preferred_element_type=jnp.float32
    )
    lane_chunk = lax.broadcasted_iota(jnp.int32, (32, 32 * CHUNKS), 1) >> 5
    gram = jnp.zeros((32, 32 * CHUNKS), jnp.float32)
    for c in range(CHUNKS):
        gram = jnp.where(lane_chunk == c, square[32 * c : 32 * c + 32, :], gram)
    gram = gram[:COLUMNS, :] + gram[COLUMNS:, :]
    tiled = exact_pick(gram, columns_alike(32 * CHUNKS, LANES))
    lanes = lax.broadcasted_iota(jnp.int32, (COLUMNS, LANES), 1)
    rows = lax.broadcasted_iota(jnp.int32, (COLUMNS, LANES), 0)
    kept = jnp.where((lanes >> 4) == (rows & 7), tiled, 0.0)
    for half in range(2):
        flat = jnp.sum(kept[8 * half : 8 * half + 8, :], axis=0, keepdims=True)
        out_ref[pl.ds(8 + half, CHIPS, stride=WIDTH), :] = jnp.broadcast_to(flat, (CHIPS, LANES))


def place_kernel(parts_ref, out_hbm, gram_hbm, out_ref, gram_ref, sems):
    copies = []
    for half in range(2):
        for quarter in range(4):
            turned = parts_ref[pl.ds(4 * half + quarter, LANES, stride=WIDTH), :].T
            for b in range(16):
                block = quarter * 16 + b
                out_ref[half, :, block * LANES : (block + 1) * LANES] = turned[
                    8 * b : 8 * b + 8, :
                ]
            if quarter % 2 == 1:
                lanes = pl.ds((quarter - 1) * 16 * LANES, 32 * LANES)
                copies.append(
                    pltpu.make_async_copy(
                        out_ref.at[half, :, lanes],
                        out_hbm.at[pl.ds(8 * half, 8), lanes],
                        sems.at[len(copies)],
                    )
                )
                copies[-1].start()
    flat = [
        jnp.sum(parts_ref[pl.ds(8 + half, CHIPS, stride=WIDTH), :], axis=0, keepdims=True)
        for half in range(2)
    ]
    lanes = lax.broadcasted_iota(jnp.int32, (COLUMNS, LANES), 1)
    rows = lax.broadcasted_iota(jnp.int32, (COLUMNS, LANES), 0)
    spread = jnp.where(rows < 8, flat[0], flat[1])
    spread = jnp.where((lanes >> 4) == (rows & 7), spread, 0.0)
    gram_ref[...] = exact_pick(spread, columns_alike(LANES, COLUMNS)) / jnp.float32(SAMPLES)
    copies.append(pltpu.make_async_copy(gram_ref, gram_hbm, sems.at[4]))
    copies[-1].start()
    for copy in copies:
        copy.wait()


def call(kernel, outs, operands, name, specs=None, out_specs=None, scratch=(), flops=0, limit=LIMIT):
    return pl.pallas_call(
        kernel,
        out_shape=outs,
        in_specs=specs or [VMEM] * len(operands),
        out_specs=out_specs or jax.tree.map(lambda _: VMEM, outs),
        scratch_shapes=scratch,
        compiler_params=pltpu.CompilerParams(vmem_limit_bytes=limit),
        cost_estimate=pl.CostEstimate(flops=flops, bytes_accessed=1 << 20, transcendentals=0),
        name=name,
    )(*operands)


def per_device(panel, signs, samples):
    f32 = jnp.float32
    whole = jax.ShapeDtypeStruct((1024, LANES), f32)
    exchange = lambda value, axes: lax.all_to_all(value, axes, 0, 0, tiled=True)
    in_hbm = lambda value: pltpu.with_memory_space_constraint(value, pltpu.HBM)
    parts, samples = call(
        local_kernel,
        (pltpu.VMEM((1024, LANES), f32), pltpu.VMEM((LANES, LANES), jnp.int32)),
        (
            in_hbm(panel),
            in_hbm(signs.reshape(BLOCKS, LANES)),
            in_hbm(samples.reshape(LANES, LANES)),
        ),
        "local_transform",
        specs=[HBM] * 3,
        scratch=[
            pltpu.VMEM((COLUMNS, LOCAL_ROWS), f32),
            pltpu.VMEM((BLOCKS, LANES), jnp.int32),
            pltpu.SemaphoreType.DMA((3,)),
        ],
    )
    parts = exchange(parts.reshape(CHIPS, 8, LANES), OUT_AXES).reshape(1024, LANES)
    parts, samples = lax.optimization_barrier((parts, samples))
    other = lax.ppermute(parts, "core", [(0, 1), (1, 0)])
    own, turned, counts = call(
        beside_kernel,
        (whole, whole, jax.ShapeDtypeStruct((2 * BLOCKS, CHIPS), f32)),
        (parts, samples),
        "own_and_counts",
        flops=1 << 30,
    )
    back = call(
        both_kernel,
        jax.ShapeDtypeStruct((CHIPS * WIDTH, LANES), f32),
        (other, own, turned, counts),
        "both_cores",
    )
    back = exchange(back.reshape(CHIPS, 1, WIDTH * LANES), BACK_AXES)
    back = back.reshape(CHIPS * WIDTH, LANES)
    return call(
        place_kernel,
        (
            jax.ShapeDtypeStruct((COLUMNS, LOCAL_ROWS), f32),
            jax.ShapeDtypeStruct((COLUMNS, COLUMNS), f32),
        ),
        (back,),
        "place_rows",
        out_specs=(HBM, HBM),
        scratch=[
            pltpu.VMEM((2, 8, LOCAL_ROWS), f32),
            pltpu.VMEM((COLUMNS, COLUMNS), f32),
            pltpu.SemaphoreType.DMA((5,)),
        ],
    )


def solution(mesh):
    wide, narrow = mesh.devices.shape
    split_mesh = Mesh(mesh.devices.reshape(wide, narrow // 2, 2), ALL_AXES)
    return jax.shard_map(
        per_device,
        mesh=split_mesh,
        in_specs=(P(None, ALL_AXES), P(ALL_AXES), P()),
        out_specs=(P(None, ALL_AXES), P()),
        check_vma=False,
    )
```
